256 devices in a mesh: role: 2 (over y_hi), pair: 2 (over core), dev: 64 (over x, z, y_lo).
Axes of the slice: x: 4, y: 4 (y_hi: 2, y_lo: 2; y = y_hi * 2 + y_lo), z: 8, core: 2. Of those that a mesh axis runs over, the one named last changes fastest.
Arguments:
- hidden_in: bfloat16 [2048, 7168], P(('role', 'pair', 'dev')), may hold values from -6 to 6
- queries: bfloat16 [2048, 8192], P(('role', 'pair', 'dev')), may hold values from -8 to 8
- new_kv: bfloat16 [2048, 512], P(('role', 'pair', 'dev')), may hold values from -6 to 6
- kv_cache: bfloat16 [4096, 256, 512], P(('role', 'pair', 'dev')), may hold values from -6 to 6
- block_counts: int32 [256, 8], P(('role', 'pair', 'dev')), may hold values from 1 to 8, 16 in all within a row
- tail_lens: int32 [2048], P(('role', 'pair', 'dev')), may hold values from 1 to 256
- block_order: int32 [256, 16], P(('role', 'pair', 'dev')), may hold values from 0 to 15, each once within a row
- out_weight: bfloat16 [8192, 7168], P(None, 'dev'), may hold values from -0.0625 to 0.0625
- norm_gain: float32 [7168], P('dev'), may hold values from 0.25 to 1.75
- gate_weight: bfloat16 [7168, 9216], P(None, 'dev'), may hold values from -0.0625 to 0.0625
- up_weight: bfloat16 [7168, 9216], P(None, 'dev'), may hold values from -0.0625 to 0.0625
- down_weight: bfloat16 [9216, 7168], P('dev'), may hold values from -0.0625 to 0.0625
Outputs:
- hidden_out: bfloat16 [2048, 7168], P(('role', 'pair', 'dev'))
The draws below stay inside these ranges and needn't reach their ends.
Inputs may be any that keep to these rules, and one draw needn't show every extreme that they name: `block_counts`: each row sums to 16 and its largest entry is 8. `block_order`: each row is a permutation of 0 .. 15.
All inputs are finite; a program needn't handle non-finite values.
Results may differ from the reference program's by a relative error of at most 0.005.
Values may be sent and summed in bfloat16 or wider, within the bound.
No kernel may reach another device: no remote copies, remote signals or barrier semaphores. Data moves between devices by JAX's collectives and lax.ppermute only.
A program may use at most 128 MiB of HBM per device.

```python
import math
import jax
import jax.numpy as jnp
import numpy as np
from jax import lax

D = 7168
FF = 9216
HQ = 32
HD = 256
BLOCK = 256
MOST_BLOCKS = 8
R_DEV = 8
N_ATT = 256
REQ = 2048
POOL_DEV = 16


def draw_queries(key, part):
    key = jax.random.fold_in(key, 11)
    values = jax.random.truncated_normal(key, -6.0, 6.0, (REQ, HQ, HD))
    return values.reshape(REQ, HQ * HD).astype(jnp.float32).astype(jnp.bfloat16)


def draw_kv_cache(key, part):
    key = jax.random.fold_in(key, 23)
    block_total = N_ATT * POOL_DEV
    values = jax.random.truncated_normal(key, -6.0, 6.0, (block_total, BLOCK, 2 * HD))
    return values.astype(jnp.float32).astype(jnp.bfloat16)


def touch_ends(result, own_key, smallest, high):
    shape = result.shape
    index_at = [jax.random.randint(jax.random.fold_in(own_key, axis), (), 0, shape[axis]) for axis in range(len(shape))]
    result = result.at[tuple(index_at)].set(smallest)
    longest = shape.index(max(shape))
    index_at[longest] = (index_at[longest] + 1) % shape[longest]
    return result.at[tuple(index_at)].set(high)


def levels(rng, extent, cuts, least, largest):
    gain, own = 1.0, jax.random.fold_in(rng, 6)
    for axis_at, blocks in cuts:
        draws = jnp.exp(jax.random.uniform(jax.random.fold_in(own, axis_at), (blocks,), jnp.float32, least / len(cuts), largest / len(cuts)))
        gain = gain * jnp.repeat(draws, extent[axis_at] // blocks).reshape([-1 if axis == axis_at else 1 for axis in range(len(extent))])
    return gain


def profile(count, total, reach, slope):
    weights = [(1 << 20) // math.isqrt(rank ** slope) + 1 for rank in range(2, count + 1)]
    rest, given = total - reach - (count - 1), [1] * (count - 1)
    while rest > 0:
        free = [i for i in range(count - 1) if given[i] < reach]
        mass, budget = sum([weights[i] for i in free]), rest
        for i in free:
            extra = min(reach - given[i], max(1, budget * weights[i] // mass), rest)
            given[i] = given[i] + extra
            rest = rest - extra
    return np.array([reach] + given)


def uneven(stream_key, amount, total, most, skew):
    if amount == 2:
        one = jax.random.randint(stream_key, (), max(1, total - most), min(most, total - 1) + 1)
        return jnp.stack([one, total - one])
    lengths = jnp.asarray(profile(amount, total, most, skew), jnp.int32)
    twos = (amount - 1) // 2
    source_of, taker = lengths[1:1 + 2 * twos:2], lengths[2:2 + 2 * twos:2]
    margin = jnp.minimum(source_of - 1, most - taker)
    shifted = jax.random.randint(jax.random.fold_in(stream_key, 1), (twos,), 0, 1 << 20) % (margin + 1)
    lengths = lengths.at[1:1 + 2 * twos:2].set(source_of - shifted).at[2:2 + 2 * twos:2].set(taker + shifted)
    return lengths[jax.random.permutation(jax.random.fold_in(stream_key, 2), amount)]


def bell_draw(key, shape, width, most, cuts=(), held_as=jnp.bfloat16):
    level = levels(key, shape, cuts, -0.22, 0.18) if cuts else 1.0
    result = jax.random.normal(key, shape, jnp.float32) * width * level
    return jnp.minimum(jnp.maximum(result, -most), most).astype(held_as)


def setup_inputs(seed: int = 0) -> dict:
    key_list = jax.random.split(jax.random.key(seed), 13)
    return {
        "hidden_in": bell_draw(key_list[0], (REQ, D), 1.0, 6.0, ((0, 256),)),
        "queries": draw_queries(jax.random.fold_in(key_list[12], 71), 0),
        "new_kv": bell_draw(key_list[2], (REQ, 2 * HD), 1.0, 6.0, ((0, 256),)),
        "kv_cache": draw_kv_cache(jax.random.fold_in(key_list[12], 71), 0),
        "block_counts": jax.vmap(lambda own: uneven(own, R_DEV, POOL_DEV, MOST_BLOCKS, 2))(jax.random.split(key_list[4], N_ATT)).reshape((N_ATT, R_DEV)).astype(jnp.int32),
        "tail_lens": touch_ends(jax.random.randint(key_list[5], (REQ,), 1, BLOCK + 1), jax.random.fold_in(key_list[5], 1), 1, BLOCK).astype(jnp.int32),
        "block_order": jax.vmap(lambda own: jax.random.permutation(own, POOL_DEV))(jax.random.split(key_list[6], N_ATT)).reshape((N_ATT, POOL_DEV)).astype(jnp.int32),
        "out_weight": bell_draw(key_list[7], (HQ * HD, D), (HQ * HD) ** -0.5, 0.0625, ((1, 64),)),
        "norm_gain": jnp.clip(1.0 + 0.15 * jax.random.normal(key_list[8], (D,), jnp.float32), 0.25, 1.75),
        "gate_weight": bell_draw(key_list[9], (D, FF), D ** -0.5, 0.0625, ((1, 64),)),
        "up_weight": bell_draw(key_list[10], (D, FF), D ** -0.5, 0.0625, ((1, 64),)),
        "down_weight": bell_draw(key_list[11], (FF, D), FF ** -0.5, 0.0625, ((0, 64),)),
    }


norm_eps = 1e-05

def attend(queries, new_kv, kv_cache, block_counts, tail_lens, block_order):
    row_count = queries.shape[0]
    pool_size, block_len, twice = kv_cache.shape
    head_size = twice // 2
    head_count = queries.shape[1] // head_size
    score_scale = head_size ** (-0.5)
    starts = jnp.cumsum(block_counts) - block_counts
    slot_ids = jnp.arange(pool_size, dtype=jnp.int32)
    position = lax.optimization_barrier(jnp.sum(jnp.where(block_order[None, :] == slot_ids[:, None], slot_ids[None, :], 0), axis=1))
    belongs = (starts[None, :] <= position[:, None]) & (position[:, None] < (starts + block_counts)[None, :])
    block_rank = position - lax.optimization_barrier(jnp.sum(jnp.where(belongs, starts[None, :], 0), axis=1))
    context = (block_counts - 1) * block_len + tail_lens
    offsets = block_rank[:, None] * block_len + jnp.arange(block_len, dtype=jnp.int32)[None, :]
    valid = jnp.transpose(belongs)[:, :, None] & (offsets[None, :, :] < context[:, None, None])
    valid = valid.reshape(row_count, pool_size * block_len)
    keys_all = kv_cache[:, :, :head_size].reshape(pool_size * block_len, head_size)
    values_all = kv_cache[:, :, head_size:].reshape(pool_size * block_len, head_size)
    query_rows = queries.reshape(row_count * head_count, head_size)
    scores = lax.dot_general(query_rows, keys_all, (((1,), (1,)), ((), ())), preferred_element_type=jnp.float32)
    scores = scores.reshape(row_count, head_count, pool_size * block_len) * score_scale
    masked = jnp.where(valid[:, None, :], scores, -jnp.inf)
    new_keys = new_kv[:, :head_size].astype(jnp.float32)
    new_vals = new_kv[:, head_size:].astype(jnp.float32)
    own_score = lax.optimization_barrier(jnp.sum(queries.reshape(row_count, head_count, head_size).astype(jnp.float32) * new_keys[:, None, :], axis=2)) * score_scale
    row_max = jnp.maximum(lax.optimization_barrier(jnp.max(masked, axis=2)), own_score)
    weights = jnp.exp(masked - row_max[:, :, None])
    own_weight = jnp.exp(own_score - row_max)
    denom_sum = lax.optimization_barrier(jnp.sum(weights, axis=2)) + own_weight
    probs = (weights / denom_sum[:, :, None]).astype(jnp.bfloat16).reshape(row_count * head_count, pool_size * block_len)
    mixed_vals = jnp.dot(probs, values_all, preferred_element_type=jnp.float32).reshape(row_count, head_count, head_size)
    mixed_vals = mixed_vals + (own_weight / denom_sum)[:, :, None] * new_vals[:, None, :]
    return mixed_vals.reshape(row_count, head_count * head_size).astype(jnp.bfloat16)

def reference(hidden_in, queries, new_kv, kv_cache, block_counts, tail_lens, block_order, out_weight, norm_gain, gate_weight, up_weight, down_weight):

    def one_device(shard_args):
        return attend(*shard_args)
    attended = lax.map(one_device, (queries.reshape(N_ATT, R_DEV, HQ * HD), new_kv.reshape(N_ATT, R_DEV, 2 * HD), kv_cache.reshape(N_ATT, POOL_DEV, BLOCK, 2 * HD), block_counts, tail_lens.reshape(N_ATT, R_DEV), block_order))
    attended = attended.reshape(REQ, HQ * HD)
    stream = hidden_in.astype(jnp.float32) + jnp.dot(attended, out_weight, preferred_element_type=jnp.float32)
    mean_square = lax.optimization_barrier(jnp.mean(stream * stream, axis=1))
    normed = (stream * lax.rsqrt(mean_square + norm_eps)[:, None] * norm_gain[None, :]).astype(jnp.bfloat16)
    gate_proj = jnp.dot(normed, gate_weight, preferred_element_type=jnp.float32)
    up_proj = jnp.dot(normed, up_weight, preferred_element_type=jnp.float32)
    hidden_act = (jax.nn.silu(gate_proj) * up_proj).astype(jnp.bfloat16)
    return (stream + jnp.dot(hidden_act, down_weight, preferred_element_type=jnp.float32)).astype(jnp.bfloat16)
```

```python
import jax
import jax.numpy as jnp
from jax import lax
from jax.sharding import Mesh, PartitionSpec as P

norm_eps = 1e-05


def attend(queries, new_kv, kv_cache, block_counts, tail_lens, block_order):
    row_count = queries.shape[0]
    pool_size, block_len, twice = kv_cache.shape
    head_size = twice // 2
    head_count = queries.shape[1] // head_size
    score_scale = head_size ** (-0.5)
    starts = jnp.cumsum(block_counts) - block_counts
    slot_ids = jnp.arange(pool_size, dtype=jnp.int32)
    position = jnp.sum(
        jnp.where(block_order[None, :] == slot_ids[:, None], slot_ids[None, :], 0), axis=1
    )
    belongs = (starts[None, :] <= position[:, None]) & (
        position[:, None] < (starts + block_counts)[None, :]
    )
    block_rank = position - jnp.sum(jnp.where(belongs, starts[None, :], 0), axis=1)
    context = (block_counts - 1) * block_len + tail_lens
    offsets = block_rank[:, None] * block_len + jnp.arange(block_len, dtype=jnp.int32)[None, :]
    valid = jnp.transpose(belongs)[:, :, None] & (offsets[None, :, :] < context[:, None, None])
    valid = valid.reshape(row_count, pool_size * block_len)
    keys_all = kv_cache[:, :, :head_size].reshape(pool_size * block_len, head_size)
    values_all = kv_cache[:, :, head_size:].reshape(pool_size * block_len, head_size)
    query_rows = queries.reshape(row_count * head_count, head_size)
    scores = lax.dot_general(
        query_rows, keys_all, (((1,), (1,)), ((), ())), preferred_element_type=jnp.float32
    )
    scores = scores.reshape(row_count, head_count, pool_size * block_len) * score_scale
    masked = jnp.where(valid[:, None, :], scores, -jnp.inf)
    new_keys = new_kv[:, :head_size].astype(jnp.float32)
    new_vals = new_kv[:, head_size:].astype(jnp.float32)
    own_score = (
        jnp.sum(
            queries.reshape(row_count, head_count, head_size).astype(jnp.float32)
            * new_keys[:, None, :],
            axis=2,
        )
        * score_scale
    )
    row_max = jnp.maximum(jnp.max(masked, axis=2), own_score)
    weights = jnp.exp(masked - row_max[:, :, None])
    own_weight = jnp.exp(own_score - row_max)
    denom_sum = jnp.sum(weights, axis=2) + own_weight
    probs = (
        (weights / denom_sum[:, :, None])
        .astype(jnp.bfloat16)
        .reshape(row_count * head_count, pool_size * block_len)
    )
    mixed_vals = jnp.dot(probs, values_all, preferred_element_type=jnp.float32).reshape(
        row_count, head_count, head_size
    )
    mixed_vals = mixed_vals + (own_weight / denom_sum)[:, :, None] * new_vals[:, None, :]
    return mixed_vals.reshape(row_count, head_count * head_size).astype(jnp.bfloat16)


def shifted(value, axis, step):
    size = lax.axis_size(axis)
    return lax.ppermute(value, axis, [(i, (i + step) % size) for i in range(size)])


def halves(weight, core):
    rows = weight.shape[0] // 2
    mine = lax.dynamic_slice_in_dim(weight, core * rows, rows, 0)
    other = lax.dynamic_slice_in_dim(weight, (1 - core) * rows, rows, 0)
    return mine, other


def spread(mine, other, pieces_for):
    got = [jnp.concatenate([pieces_for(mine, 0), pieces_for(other, 0)], axis=0)]
    for step in range(1, X):
        near = shifted(pieces_for(mine, step), "x", step)
        far = shifted(near, "pair", 1)
        got.append(jnp.concatenate([near, far], axis=0))
    return got


X, Z, Y = 4, 8, 2


def per_device(
    hidden_in,
    queries,
    new_kv,
    kv_cache,
    block_counts,
    tail_lens,
    block_order,
    out_weight,
    norm_gain,
    gate_weight,
    up_weight,
    down_weight,
):
    f32, bf16 = jnp.float32, jnp.bfloat16
    core, at_x, at_z, at_y = (lax.axis_index(a) for a in ("pair", "x", "z", "y"))
    rows, width = hidden_in.shape
    line = Z * Y
    cols = width // (X * line)
    chunk = rows * line
    slab = width // X
    ff = gate_weight.shape[1]

    out_t = spread(*halves(out_weight.T, core), lambda w, step: w)

    def slab_of(step):
        begin = ((at_x + step) % X) * slab
        return lambda w: lax.dynamic_slice_in_dim(w, begin, slab, 1)

    gate_h, up_h = halves(gate_weight.T, core), halves(up_weight.T, core)
    gate_up = spread(
        (gate_h[0], up_h[0]),
        (gate_h[1], up_h[1]),
        lambda w, step: jnp.concatenate([slab_of(step)(w[0]), slab_of(step)(w[1])], axis=0),
    )
    down = spread(*halves(down_weight, core), lambda w, step: w)

    attended = attend(queries, new_kv, kv_cache, block_counts[0], tail_lens, block_order[0])

    resid = hidden_in.reshape(rows, X, line, cols)
    resid = jnp.stack(
        [lax.dynamic_index_in_dim(resid, (at_x - d) % X, 1, keepdims=False) for d in range(X)], axis=2
    )
    resid = jnp.pad(resid, ((0, 0), (0, 0), (0, 0), (0, 128 - cols)))
    resid = resid.transpose(1, 0, 2, 3).reshape(line, rows, X * 128)
    first = jnp.concatenate(
        [jnp.broadcast_to(attended[None], (line,) + attended.shape), resid], axis=2
    )
    first = lax.all_to_all(first, ("z", "y"), 0, 0, tiled=True)
    heads = first[:, :, : attended.shape[1]].reshape(chunk, attended.shape[1])
    resid = first[:, :, attended.shape[1] :].reshape(chunk, X, 128)[:, :, :cols]
    resid = resid.transpose(1, 2, 0).astype(f32)

    proj = lax.dot_general(
        jnp.concatenate(out_t, axis=0), heads, (((1,), (1,)), ((), ())), preferred_element_type=f32
    ).reshape(X, 2, cols // 2, chunk)
    proj = jnp.where(core == 0, proj, proj[:, ::-1]).reshape(X, cols, chunk)
    part = proj + resid
    stream = jnp.stack(
        [part[0]] + [shifted(part[d], "x", -d) for d in range(1, X)], axis=1
    ).reshape(cols, X * chunk)
    squares = jnp.sum(stream * stream, axis=0)
    high = squares.astype(bf16)
    low = (squares - high.astype(f32)).astype(bf16)
    scaled = (stream * norm_gain[:, None]).astype(bf16)
    second = jnp.concatenate(
        [scaled, high[None], low[None], jnp.zeros((6, X * chunk), bf16)], axis=0
    )
    second = lax.all_to_all(
        jnp.broadcast_to(second[None], (line,) + second.shape), ("z", "y"), 0, 0, tiled=True
    )
    squares = jnp.sum(second[:, cols : cols + 2].astype(f32), axis=(0, 1))
    scaled = second[:, :cols].reshape(slab, X * chunk)

    halved = [
        jnp.dot(w, scaled, preferred_element_type=f32) for w in gate_up
    ]
    total, square_total = 0.0, 0.0
    for step in range(X):
        here = slice(step * chunk, (step + 1) * chunk)
        blocks = [halved[(d - step) % X][:, here] for d in range(X)]
        sq = squares[here]
        if step == 0:
            total = jnp.concatenate(blocks, axis=0)
            square_total = sq
        else:
            high = sq.astype(bf16)
            low = (sq - high.astype(f32)).astype(bf16)
            send = jnp.concatenate(
                [b.astype(bf16) for b in blocks]
                + [high[None], low[None], jnp.zeros((6, chunk), bf16)],
                axis=0,
            )
            send = shifted(send, "x", step).astype(f32)
            total = total + send[: X * 2 * ff]
            square_total = square_total + send[X * 2 * ff] + send[X * 2 * ff + 1]
    scale = lax.rsqrt(square_total / width + norm_eps)
    total = (total * scale[None, :]).reshape(X * 2, 2, ff // 2, chunk)
    hidden = (jax.nn.silu(total[:, 0]) * total[:, 1]).astype(bf16).reshape(X * ff, chunk)

    spots = ((at_x - jnp.arange(X)) % X) * line + at_z * Y + at_y
    spots = (spots[:, None] * cols + jnp.arange(cols)[None, :]).reshape(X * cols)
    place = (spots[:, None] == jnp.arange(width)[None, :]).astype(bf16)
    result = lax.dot_general(
        jnp.concatenate([hidden, proj.reshape(X * cols, chunk).astype(bf16)], axis=0),
        jnp.concatenate(down + [place], axis=0),
        (((0,), (0,)), ((), ())),
        preferred_element_type=f32,
    ).astype(bf16)
    result = lax.all_to_all(result.reshape(line, rows, width), ("z", "y"), 0, 0, tiled=True)
    result = jnp.sum(result.astype(f32), axis=0) + hidden_in.astype(f32)
    return result.astype(bf16)


def solution(mesh):
    fine = Mesh(mesh.devices.reshape(2, 2, X, Z, Y), ("role", "pair", "x", "z", "y"))
    dev = ("x", "z", "y")
    every = ("role", "pair") + dev
    return jax.shard_map(
        per_device,
        mesh=fine,
        in_specs=(
            P(every, None),
            P(every, None),
            P(every, None),
            P(every, None, None),
            P(every, None),
            P(every),
            P(every, None),
            P(None, dev),
            P(dev),
            P(None, dev),
            P(None, dev),
            P(dev, None),
        ),
        out_specs=P(every, None),
        check_vma=False,
    )
```

```python
import jax
import jax.numpy as jnp
from jax import lax
from jax.experimental import pallas as pl
from jax.experimental.pallas import tpu as pltpu
from jax.sharding import Mesh, PartitionSpec as P

norm_eps = 1e-05
X, Z, Y = 4, 8, 2
LINE = Z * Y
f32, bf16 = jnp.float32, jnp.bfloat16
NT = (((1,), (1,)), ((), ()))
VMEM_LIMIT = 48 * 1024 * 1024


def smem():
    return pl.BlockSpec(memory_space=pltpu.SMEM)


def vmem():
    return pl.BlockSpec(memory_space=pltpu.VMEM)


def anywhere():
    return pl.BlockSpec(memory_space=pl.ANY)


def call(kernel, outs, ins, scratch, cost):
    single = not isinstance(outs, (list, tuple))
    return pl.pallas_call(
        kernel,
        out_shape=outs,
        in_specs=ins,
        out_specs=vmem() if single else [vmem()] * len(outs),
        scratch_shapes=scratch,
        compiler_params=pltpu.CompilerParams(vmem_limit_bytes=VMEM_LIMIT),
        cost_estimate=pl.CostEstimate(flops=cost[0], bytes_accessed=cost[1], transcendentals=0),
    )


def attend_kernel(counts, tails, order, q_ref, new_ref, kv_ref, out_ref, score, top, total, mixed):
    rows, heads, size = q_ref.shape
    pool, block, _ = kv_ref.shape
    scale = size ** (-0.5)
    owner, limit = [], []
    row, rank = jnp.int32(0), jnp.int32(0)
    for p in range(pool):
        last = rank + 1 == counts[0, row]
        owner.append(row)
        limit.append(jnp.where(last, tails[row], block))
        row = jnp.minimum(jnp.where(last, row + 1, row), rows - 1)
        rank = jnp.where(last, 0, rank + 1)
    own = []
    for r in range(rows):
        key = new_ref[r : r + 1, :size].astype(f32)
        own.append(jnp.sum(q_ref[r].astype(f32) * key, axis=1, keepdims=True) * scale)
        top[r] = jnp.broadcast_to(own[r], (heads, 128))
    lane = lax.broadcasted_iota(jnp.int32, (heads, block), 1)
    for p in range(pool):
        s = lax.dot_general(
            q_ref[owner[p]], kv_ref[order[0, p], :, :size], NT, preferred_element_type=f32
        )
        s = jnp.where(lane < limit[p], s * scale, -jnp.inf)
        score[p] = s
        top[owner[p]] = jnp.maximum(top[owner[p]], jnp.max(s, axis=1, keepdims=True))
    for r in range(rows):
        weight = jnp.exp(own[r] - top[r][:, :1])
        total[r] = jnp.broadcast_to(weight, (heads, 128))
        mixed[r] = weight * new_ref[r : r + 1, size:].astype(f32)
    for p in range(pool):
        weight = jnp.exp(score[p] - top[owner[p]][:, :1])
        total[owner[p]] += jnp.sum(weight, axis=1, keepdims=True)
        mixed[owner[p]] += jnp.dot(
            weight.astype(bf16), kv_ref[order[0, p], :, size:], preferred_element_type=f32
        )
    for r in range(rows):
        out_ref[r] = (mixed[r] / total[r][:, :1]).astype(bf16)


def attend(queries, new_kv, kv_cache, block_counts, tail_lens, block_order):
    rows = queries.shape[0]
    pool, block, twice = kv_cache.shape
    size = twice // 2
    heads = queries.shape[1] // size
    mixed = call(
        attend_kernel,
        jax.ShapeDtypeStruct((rows, heads, size), bf16),
        [smem()] * 3 + [vmem()] * 3,
        [
            pltpu.VMEM((pool, heads, block), f32),
            pltpu.VMEM((rows, heads, 128), f32),
            pltpu.VMEM((rows, heads, 128), f32),
            pltpu.VMEM((rows, heads, size), f32),
        ],
        (4 * pool * heads * block * size, pool * block * twice * 2),
    )(block_counts, tail_lens, block_order, queries.reshape(rows, heads, size), new_kv, kv_cache)
    return mixed.reshape(rows, heads * size)


def start_all(copies):
    for copy in copies:
        copy.start()
    return copies


def project_kernel(core, first, w0, w1, w2, w3, w4, w5, w6, proj_out, part_out, weight, sems):
    width = w0.shape[1]
    cols = w0.shape[0]
    half = width // 2
    mine = pl.multiple_of(core[0] * half, 128)
    other = pl.multiple_of((1 - core[0]) * half, 128)
    copies = [pltpu.make_async_copy(w0, weight.at[pl.ds(0, cols)], sems.at[0])]
    for d, (near, far) in enumerate(((w1, w2), (w3, w4), (w5, w6)), 1):
        rows = pl.ds(d * cols, cols)
        copies.append(
            pltpu.make_async_copy(near, weight.at[rows, pl.ds(mine, half)], sems.at[2 * d - 1])
        )
        copies.append(
            pltpu.make_async_copy(far, weight.at[rows, pl.ds(other, half)], sems.at[2 * d])
        )
    start_all(copies)
    for copy in copies:
        copy.wait()
    step = 1024

    def body(i, acc):
        at = pl.ds(pl.multiple_of(i * step, 128), step)
        return acc + lax.dot_general(weight[:, at], first[:, at], NT, preferred_element_type=f32)

    proj = lax.fori_loop(0, width // step, body, jnp.zeros((X * cols, first.shape[0]), f32))
    for d in range(X):
        here = proj[d * cols : (d + 1) * cols]
        proj_out[d] = here.astype(bf16)
        resid = first[:, width + d * 128 : width + (d + 1) * 128].astype(f32).T
        part_out[d] = here + resid[:cols]


def gate_up_kernel(
    place, second, gate, up, w1, w2, w3, w4, w5, w6, own_out, square_out, o1, o2, o3, weight, normed, sems
):
    ff = gate.shape[0]
    cols = normed.shape[0] // LINE
    slab = normed.shape[0]
    half = slab // 2
    chunk = normed.shape[1] // X
    mine = pl.multiple_of(place[0] * half, 128)
    other = pl.multiple_of((1 - place[0]) * half, 128)
    begin = pl.multiple_of(place[1] * slab, 128)
    copies = [
        pltpu.make_async_copy(gate.at[:, pl.ds(begin, slab)], weight.at[pl.ds(0, ff)], sems.at[0]),
        pltpu.make_async_copy(up.at[:, pl.ds(begin, slab)], weight.at[pl.ds(ff, ff)], sems.at[1]),
    ]
    for d, (near, far) in enumerate(((w1, w2), (w3, w4), (w5, w6)), 1):
        rows = pl.ds(d * 2 * ff, 2 * ff)
        copies.append(
            pltpu.make_async_copy(near, weight.at[rows, pl.ds(mine, half)], sems.at[2 * d])
        )
        copies.append(
            pltpu.make_async_copy(far, weight.at[rows, pl.ds(other, half)], sems.at[2 * d + 1])
        )
    for i in range(LINE):
        to = i % Z * Y + i // Z
        copies.append(
            pltpu.make_async_copy(
                second.at[i, pl.ds(0, cols)], normed.at[pl.ds(to * cols, cols)], sems.at[8 + i]
            )
        )
    start_all(copies)
    squares = jnp.sum(second[:, cols : cols + 8].astype(f32), axis=0)
    squares = squares[0:1] + squares[1:2]
    for copy in copies:
        copy.wait()
    outs = (own_out, o1, o2, o3)
    for d in range(X):
        rows = slice(d * 2 * ff, (d + 1) * 2 * ff)
        got = jnp.dot(weight[rows], normed[...], preferred_element_type=f32)
        for e in range(X):
            to = (d + e) % X
            outs[e][to * 2 * ff : (to + 1) * 2 * ff] = got[:, e * chunk : (e + 1) * chunk].astype(
                outs[e].dtype
            )
    square_out[...] = squares[:, :chunk]
    line = lax.broadcasted_iota(jnp.int32, (8, chunk), 0)
    for e in range(1, X):
        here = squares[:, e * chunk : (e + 1) * chunk]
        high = here.astype(bf16).astype(f32)
        both = jnp.where(line == 0, high, jnp.where(line == 1, here - high, 0.0))
        outs[e][X * 2 * ff :] = both.astype(bf16)


def down_kernel(
    place, own, square, r1, r2, r3, proj, w0, w1, w2, w3, w4, w5, w6, out, weight, total, sems
):
    ff, width = w0.shape
    half = width // 2
    chunk = out.shape[0]
    cols = proj.shape[1]
    mine = pl.multiple_of(place[0] * half, 128)
    other = pl.multiple_of((1 - place[0]) * half, 128)
    copies = [pltpu.make_async_copy(w0, weight.at[pl.ds(0, ff)], sems.at[0])]
    for d, (near, far) in enumerate(((w1, w2), (w3, w4), (w5, w6)), 1):
        rows = pl.ds(d * ff, ff)
        copies.append(
            pltpu.make_async_copy(near, weight.at[rows, pl.ds(mine, half)], sems.at[2 * d - 1])
        )
        copies.append(
            pltpu.make_async_copy(far, weight.at[rows, pl.ds(other, half)], sems.at[2 * d])
        )
    start_all(copies)
    end = X * 2 * ff
    squares = square[...]
    for r in (r1, r2, r3):
        tail = r[end:].astype(f32)
        squares = squares + tail[0:1] + tail[1:2]
    scale = lax.rsqrt(squares / width + norm_eps)
    hidden = []
    for d in range(X):
        at = d * 2 * ff
        gate, up = (
            (
                own[a : a + ff]
                + r1[a : a + ff].astype(f32)
                + r2[a : a + ff].astype(f32)
                + r3[a : a + ff].astype(f32)
            )
            * scale
            for a in (at, at + ff)
        )
        hidden.append((gate / (1.0 + jnp.exp(-gate)) * up).T.astype(bf16))
    hidden = jnp.concatenate(hidden, axis=1)
    for copy in copies:
        copy.wait()
    step = 1024

    def body(i, _):
        at = pl.ds(pl.multiple_of(i * step, 128), step)
        total[:, at] = jnp.dot(hidden, weight[:, at], preferred_element_type=f32)
        return 0

    lax.fori_loop(0, width // step, body, 0)
    row = lax.broadcasted_iota(jnp.int32, (cols, 256), 0)
    lane = lax.broadcasted_iota(jnp.int32, (cols, 256), 1)
    for d in range(X):
        spot = place[1 + d]
        base = jnp.minimum(spot // 128 * 128, width - 256)
        pick = (row + (spot - base) == lane).astype(bf16)
        at = pl.ds(pl.multiple_of(base, 128), 256)
        total[:, at] += lax.dot_general(
            proj[d], pick, (((0,), (0,)), ((), ())), preferred_element_type=f32
        )
    out[...] = total[...].astype(bf16)


def shifted(value, axis, step):
    size = lax.axis_size(axis)
    return lax.ppermute(value, axis, [(i, (i + step) % size) for i in range(size)])


def send_along_x(pieces):
    return [shifted(piece, "x", step) for step, piece in enumerate(pieces, 1)]


def with_other_core(near):
    both = []
    for piece in near:
        both += [piece, shifted(piece, "pair", 1)]
    return both


def after(values, *others):
    return lax.optimization_barrier((values, others))[0]


def per_device(
    hidden_in,
    queries,
    new_kv,
    kv_cache,
    block_counts,
    tail_lens,
    block_order,
    out_weight,
    norm_gain,
    gate_weight,
    up_weight,
    down_weight,
):
    core, at_x, at_z, at_y = (lax.axis_index(a) for a in ("pair", "x", "z", "y"))
    rows, width = hidden_in.shape
    cols = width // (X * LINE)
    chunk = rows * LINE
    slab = width // X
    ff = gate_weight.shape[1]
    heads_width = queries.shape[1]
    out_t, gate_t, up_t = out_weight.T, gate_weight.T, up_weight.T

    def lanes(weight, begin, size):
        return lax.dynamic_slice_in_dim(weight, begin, size, 1)

    piece = lanes(out_t, core * (heads_width // 2), heads_width // 2)
    out_near = send_along_x([piece] * (X - 1))

    attended = attend(queries, new_kv, kv_cache, block_counts, tail_lens, block_order)
    resid = hidden_in.reshape(rows, X, LINE, cols)
    resid = jnp.stack(
        [lax.dynamic_index_in_dim(resid, (at_x - d) % X, 1, keepdims=False) for d in range(X)], axis=2
    )
    resid = jnp.pad(resid, ((0, 0), (0, 0), (0, 0), (0, 128 - cols)))
    resid = resid.reshape(rows, Z, Y, X * 128).transpose(2, 1, 0, 3).reshape(LINE, rows, X * 128)
    first = jnp.concatenate(
        [jnp.broadcast_to(attended[None], (LINE,) + attended.shape), resid], axis=2
    )
    first = lax.all_to_all(first, ("y", "z"), 0, 0, tiled=True)
    first = first.reshape(chunk, heads_width + X * 128)

    gate_t, up_t = after((gate_t, up_t), out_near)
    pieces = []
    for step in range(1, X):
        begin = ((at_x + step) % X) * slab + core * (slab // 2)
        pieces.append(
            jnp.concatenate(
                [lanes(gate_t, begin, slab // 2), lanes(up_t, begin, slab // 2)], axis=0
            )
        )
    gate_up_near = send_along_x(pieces)
    down_weight = after(down_weight, gate_up_near)
    piece = lanes(down_weight, core * (width // 2), width // 2)
    down_near = send_along_x([piece] * (X - 1))

    proj, part = call(
        project_kernel,
        [
            jax.ShapeDtypeStruct((X, cols, chunk), bf16),
            jax.ShapeDtypeStruct((X, cols, chunk), f32),
        ],
        [smem(), vmem()] + [anywhere()] * 7,
        [pltpu.VMEM((X * cols, heads_width), bf16), pltpu.SemaphoreType.DMA((7,))],
        (2 * X * cols * chunk * heads_width, X * cols * heads_width * 4),
    )(core.reshape(1), first, out_t, *with_other_core(out_near))

    stream = jnp.stack(
        [part[0]] + [shifted(part[d], "x", -d) for d in range(1, X)], axis=1
    ).reshape(cols, X * chunk)
    squares = jnp.sum(stream * stream, axis=0)
    high = squares.astype(bf16)
    low = (squares - high.astype(f32)).astype(bf16)
    scaled = (stream * norm_gain[:, None]).astype(bf16)
    second = jnp.concatenate(
        [scaled, high[None], low[None], jnp.zeros((6, X * chunk), bf16)], axis=0
    )
    second = lax.all_to_all(
        jnp.broadcast_to(second[None], (LINE,) + second.shape), ("y", "z"), 0, 0, tiled=True
    )

    message = jax.ShapeDtypeStruct((X * 2 * ff + 8, chunk), bf16)
    own, square, *sends = call(
        gate_up_kernel,
        [
            jax.ShapeDtypeStruct((X * 2 * ff, chunk), f32),
            jax.ShapeDtypeStruct((1, chunk), f32),
            message,
            message,
            message,
        ],
        [smem(), vmem()] + [anywhere()] * 8,
        [
            pltpu.VMEM((X * 2 * ff, slab), bf16),
            pltpu.VMEM((slab, X * chunk), bf16),
            pltpu.SemaphoreType.DMA((8 + LINE,)),
        ],
        (4 * X * ff * slab * X * chunk, X * 2 * ff * slab * 4),
    )(jnp.stack([core, at_x]), second, gate_t, up_t, *with_other_core(gate_up_near))
    received = send_along_x(sends)

    spots = [(((at_x - d) % X) * LINE + at_z * Y + at_y) * cols for d in range(X)]
    result = call(
        down_kernel,
        jax.ShapeDtypeStruct((chunk, width), bf16),
        [smem()] + [vmem()] * 6 + [anywhere()] * 7,
        [
            pltpu.VMEM((X * ff, width), bf16),
            pltpu.VMEM((chunk, width), f32),
            pltpu.SemaphoreType.DMA((7,)),
        ],
        (2 * X * ff * chunk * width, X * ff * width * 4),
    )(
        jnp.stack([core] + spots),
        own,
        square,
        *received,
        proj,
        down_weight,
        *with_other_core(down_near),
    )
    result = lax.all_to_all(result.reshape(LINE, rows, width), ("y", "z"), 0, 0, tiled=True)
    result = jnp.sum(result.astype(f32), axis=0) + hidden_in.astype(f32)
    return result.astype(bf16)


def solution(mesh):
    fine = Mesh(mesh.devices.reshape(2, 2, X, Z, Y), ("role", "pair", "x", "z", "y"))
    dev = ("x", "z", "y")
    every = ("role", "pair") + dev
    return jax.shard_map(
        per_device,
        mesh=fine,
        in_specs=(
            P(every, None),
            P(every, None),
            P(every, None),
            P(every, None, None),
            P(every, None),
            P(every),
            P(every, None),
            P(None, dev),
            P(dev),
            P(None, dev),
            P(None, dev),
            P(dev, None),
        ),
        out_specs=P(every, None),
        check_vma=False,
    )
```

```python
import jax
import jax.numpy as jnp
from jax import lax
from jax.experimental import pallas as pl
from jax.experimental.pallas import tpu as pltpu
from jax.sharding import Mesh, PartitionSpec as P

norm_eps = 1e-05
X, Z, Y = 4, 8, 2
LINE = Z * Y
f32, bf16 = jnp.float32, jnp.bfloat16
NT = (((1,), (1,)), ((), ()))
VMEM_LIMIT = 58 * 1024 * 1024


def smem():
    return pl.BlockSpec(memory_space=pltpu.SMEM)


def vmem():
    return pl.BlockSpec(memory_space=pltpu.VMEM)


def anywhere():
    return pl.BlockSpec(memory_space=pl.ANY)


def call(kernel, outs, ins, scratch, cost):
    single = not isinstance(outs, (list, tuple))
    return pl.pallas_call(
        kernel,
        out_shape=outs,
        in_specs=ins,
        out_specs=vmem() if single else [vmem()] * len(outs),
        scratch_shapes=scratch,
        compiler_params=pltpu.CompilerParams(vmem_limit_bytes=VMEM_LIMIT),
        cost_estimate=pl.CostEstimate(flops=cost[0], bytes_accessed=cost[1], transcendentals=0),
    )


def attend_kernel(counts, tails, order, q_ref, new_ref, kv_ref, out_ref, score, top, total, mixed):
    rows, heads, size = q_ref.shape
    pool, block, _ = kv_ref.shape
    scale = size ** (-0.5)
    owner, limit = [], []
    row, rank = jnp.int32(0), jnp.int32(0)
    for p in range(pool):
        last = rank + 1 == counts[0, row]
        owner.append(row)
        limit.append(jnp.where(last, tails[row], block))
        row = jnp.minimum(jnp.where(last, row + 1, row), rows - 1)
        rank = jnp.where(last, 0, rank + 1)
    own = []
    for r in range(rows):
        key = new_ref[r : r + 1, :size].astype(f32)
        own.append(jnp.sum(q_ref[r].astype(f32) * key, axis=1, keepdims=True) * scale)
        top[r] = jnp.broadcast_to(own[r], (heads, 128))
    lane = lax.broadcasted_iota(jnp.int32, (heads, block), 1)
    for p in range(pool):
        s = lax.dot_general(
            q_ref[owner[p]], kv_ref[order[0, p], :, :size], NT, preferred_element_type=f32
        )
        s = jnp.where(lane < limit[p], s * scale, -jnp.inf)
        score[p] = s
        top[owner[p]] = jnp.maximum(top[owner[p]], jnp.max(s, axis=1, keepdims=True))
    for r in range(rows):
        weight = jnp.exp(own[r] - top[r][:, :1])
        total[r] = jnp.broadcast_to(weight, (heads, 128))
        mixed[r] = weight * new_ref[r : r + 1, size:].astype(f32)
    for p in range(pool):
        weight = jnp.exp(score[p] - top[owner[p]][:, :1])
        total[owner[p]] += jnp.sum(weight, axis=1, keepdims=True)
        mixed[owner[p]] += jnp.dot(
            weight.astype(bf16), kv_ref[order[0, p], :, size:], preferred_element_type=f32
        )
    for r in range(rows):
        out_ref[r] = (mixed[r] / total[r][:, :1]).astype(bf16)


def attend(queries, new_kv, kv_cache, block_counts, tail_lens, block_order):
    rows = queries.shape[0]
    pool, block, twice = kv_cache.shape
    size = twice // 2
    heads = queries.shape[1] // size
    mixed = call(
        attend_kernel,
        jax.ShapeDtypeStruct((rows, heads, size), bf16),
        [smem()] * 3 + [vmem()] * 3,
        [
            pltpu.VMEM((pool, heads, block), f32),
            pltpu.VMEM((rows, heads, 128), f32),
            pltpu.VMEM((rows, heads, 128), f32),
            pltpu.VMEM((rows, heads, size), f32),
        ],
        (4 * pool * heads * block * size, pool * block * twice * 2),
    )(block_counts, tail_lens, block_order, queries.reshape(rows, heads, size), new_kv, kv_cache)
    return mixed.reshape(rows, heads * size)


def gather_pieces(pieces, sems):
    copies = [
        pltpu.make_async_copy(source, target, sems.at[i]) for i, (source, target) in enumerate(pieces)
    ]
    for copy in copies:
        copy.start()
    return copies


def wait_all(copies):
    for copy in copies:
        copy.wait()


def offset(value, unit):
    return pl.multiple_of(value, unit)


def project_kernel(at, first, near, near_far, side, side_far, own_out, o1, o2, o3, weight, sems):
    core, at_y = at[0], at[3]
    cols, half = near.shape[0] // X, near.shape[1]
    width = 2 * half
    pieces = []
    for which, y in ((near, at_y), (side, 1 - at_y)):
        rows = pl.ds(offset(y * X * cols, 16), X * cols)
        pieces.append((which, weight.at[rows, pl.ds(offset(core * half, 128), half)]))
    for which, y in ((near_far, at_y), (side_far, 1 - at_y)):
        rows = pl.ds(offset(y * X * cols, 16), X * cols)
        pieces.append((which, weight.at[rows, pl.ds(offset((1 - core) * half, 128), half)]))
    wait_all(gather_pieces(pieces, sems))
    for y in range(Y):
        for d, out in enumerate((own_out, o1, o2, o3)):
            rows = slice((y * X + d) * cols, (y * X + d + 1) * cols)
            got = lax.dot_general(
                weight[rows], first[:, :width], NT, preferred_element_type=f32
            )
            out[y * cols : (y + 1) * cols] = got.astype(out.dtype)


def norm_kernel(first, own, r1, r2, r3, gain, second, proj_out):
    cols = own.shape[0]
    width = first.shape[1] - 256
    proj = own[...] + r1[...].astype(f32) + r2[...].astype(f32) + r3[...].astype(f32)
    resid = first[:, width:].astype(f32).T
    stream = proj + resid[:cols]
    squares = jnp.sum(stream * stream, axis=0, keepdims=True)
    high = squares.astype(bf16).astype(f32)
    line = lax.broadcasted_iota(jnp.int32, (8, stream.shape[1]), 0)
    tail = jnp.where(line == 0, high, jnp.where(line == 1, squares - high, 0.0)).astype(bf16)
    scaled = (stream * gain[...]).astype(bf16)
    for z in range(Z):
        second[z, :cols] = scaled
        second[z, cols:] = tail
    proj_out[...] = jnp.concatenate(
        [proj, jnp.zeros((256 - cols, proj.shape[1]), f32)], axis=0
    ).T


def gate_up_kernel(
    at, second, proj, near, near_far, side, side_far, own_out, o1, o2, o3, weight, normed, total, sems
):
    core, at_x, at_y = at[0], at[1], at[3]
    ff2, half = near.shape[0] // X, near.shape[1]
    ff = ff2 // 2
    span = X * Y * ff
    cols = normed.shape[0] // Z
    pieces = []
    for which, c, y in (
        (near, core, at_y),
        (side, core, 1 - at_y),
        (near_far, 1 - core, at_y),
        (side_far, 1 - core, 1 - at_y),
    ):
        lanes = pl.ds(offset(c * half, 128), half)
        for d in range(X):
            block = (y * X + (at_x + X - d) % X) * ff
            for part in range(2):
                pieces.append(
                    (
                        which.at[pl.ds(d * ff2 + part * ff, ff)],
                        weight.at[pl.ds(offset(part * span + block, 16), ff), lanes],
                    )
                )
    for z in range(Z):
        pieces.append((second.at[z, pl.ds(0, cols)], normed.at[pl.ds(z * cols, cols)]))
    copies = gather_pieces(pieces, sems)
    squares = jnp.sum(second[:, cols : cols + 8].astype(f32), axis=0).T
    squares = squares[:, 0:1] + squares[:, 1:2]
    high = squares.astype(bf16).astype(f32)
    lane = lax.broadcasted_iota(jnp.int32, proj.shape, 1)
    total[:, 2 * span :] = jnp.where(
        lane == cols, high, jnp.where(lane == cols + 1, squares - high, proj[...])
    )
    wait_all(copies)
    step = 384

    def body(i, _):
        rows = pl.ds(offset(i * step, 128), step)
        total[:, rows] = jnp.dot(weight[rows], normed[...], preferred_element_type=f32).T
        return 0

    lax.fori_loop(0, 2 * span // step, body, 0)
    for e, out in enumerate((own_out, o1, o2, o3)):
        to = (at_x + e) % X
        for z in range(0, Z, 2):
            pair = [total[pl.ds(offset(((z + i) * X + to) * 8, 8), 8)] for i in range(2)]
            out[z * 8 : (z + 2) * 8] = jnp.concatenate(pair, axis=0).astype(out.dtype)


def act_kernel(at, width, own, r1, r2, r3, keep, send, shares):
    at_x, at_y = at[1], at[3]
    span = keep.shape[1] - 512
    summed = own[...] + r1[...].astype(f32) + r2[...].astype(f32) + r3[...].astype(f32)
    for e, r in enumerate((own, r1, r2, r3)):
        shares[e] = r[:, 2 * span :].astype(bf16)
    cols = 2 * span + 224
    squares = summed[:, cols : cols + 1] + summed[:, cols + 1 : cols + 2]
    scale = lax.rsqrt(squares / width + norm_eps)
    gate, up = summed[:, :span] * scale, summed[:, span : 2 * span] * scale
    hidden = (gate / (1.0 + jnp.exp(-gate)) * up).astype(bf16)
    for out, y in ((keep, at_y), (send, 1 - at_y)):
        out[:, :span] = hidden
        for j in range(2):
            e = (at_x + X - (2 * y + j)) % X
            out[:, span + j * 256 : span + (j + 1) * 256] = shares[e]


def down_kernel(at, keep, other, near, far, out, weight, act, total, sems):
    core, at_x, at_z, at_y = at[0], at[1], at[2], at[3]
    rows = keep.shape[0]
    half = near.shape[1]
    width = 2 * half
    ff = near.shape[0] // (X * Y)
    span = X * Y * ff
    pieces = []
    for which, c in ((near, core), (far, 1 - core)):
        lanes = pl.ds(offset(c * half, 128), half)
        for d in range(X):
            for side in range(Y):
                y = at_y if side == 0 else 1 - at_y
                block = (y * X + (at_x + X - d) % X) * ff
                pieces.append(
                    (
                        which.at[pl.ds((d * Y + side) * ff, ff)],
                        weight.at[pl.ds(offset(block, 16), ff), lanes],
                    )
                )
    copies = gather_pieces(pieces, sems)
    act[pl.ds(offset(at_y * rows, 16), rows)] = keep[...]
    act[pl.ds(offset((1 - at_y) * rows, 16), rows)] = other[...]
    wait_all(copies)
    step = 512

    def body(i, _):
        lanes = pl.ds(offset(i * step, 128), step)
        total[:, lanes] = jnp.dot(act[:, :span], weight[:, lanes], preferred_element_type=f32)
        return 0

    lax.fori_loop(0, width // step, body, 0)
    row = lax.broadcasted_iota(jnp.int32, (256, 384), 0)
    lane = lax.broadcasted_iota(jnp.int32, (256, 384), 1)
    for j in range(2):
        spot = j * half + at_z * 224
        base = jnp.minimum(spot // 128 * 128, width - 384)
        pick = jnp.where(row < 224, (row + (spot - base) == lane).astype(f32), 0.0).astype(bf16)
        lanes = pl.ds(offset(base, 128), 384)
        total[:, lanes] += jnp.dot(
            act[:, span + j * 256 : span + (j + 1) * 256], pick, preferred_element_type=f32
        )
    for z in range(Z):
        both = [total[y * rows + z * 8 : y * rows + (z + 1) * 8] for y in range(Y)]
        out[z] = jnp.concatenate(both, axis=0).astype(bf16)


def shifted(value, axis, step):
    size = lax.axis_size(axis)
    return lax.ppermute(value, axis, [(i, (i + step) % size) for i in range(size)])


def after(values, *others):
    return lax.optimization_barrier((values, others))[0]


def lanes(weight, begin, size):
    return lax.dynamic_slice_in_dim(weight, begin, size, 1)


def per_device(
    hidden_in,
    queries,
    new_kv,
    kv_cache,
    block_counts,
    tail_lens,
    block_order,
    out_weight,
    norm_gain,
    gate_weight,
    up_weight,
    down_weight,
):
    core, at_x, at_z, at_y = (lax.axis_index(a) for a in ("pair", "x", "z", "y"))
    at = jnp.stack([core, at_x, at_z, at_y])
    rows, width = hidden_in.shape
    slab = width // X
    block = width // (X * Z * Y)
    cols = Y * block
    chunk = X * Z * rows
    ff = gate_weight.shape[1]
    span = X * Y * ff
    heads = queries.shape[1] // X
    out_t, gate_t, up_t = out_weight.T, gate_weight.T, up_weight.T

    half = heads // 2
    pieces = [lanes(out_t, (at_x + d) % X * heads + core * half, half) for d in range(X)]
    out_near = jnp.concatenate(
        [pieces[0]] + [shifted(pieces[d], "x", d) for d in range(1, X)], axis=0
    )
    gain = shifted(norm_gain, "y", 1)
    gain = jnp.where(
        at_y == 0, jnp.concatenate([norm_gain, gain]), jnp.concatenate([gain, norm_gain])
    )[:, None]

    attended = attend(queries, new_kv, kv_cache, block_counts, tail_lens, block_order)
    first = jnp.concatenate(
        [attended.reshape(rows, X, heads), hidden_in.reshape(rows, X, slab)], axis=2
    ).transpose(1, 0, 2)
    first = after(first, out_near)
    first = lax.all_to_all(first, "x", 0, 0, tiled=True).reshape(X * rows, heads + slab)
    resid = first[:, heads:].reshape(X * rows, Z, cols).transpose(1, 0, 2)
    resid = jnp.pad(resid, ((0, 0), (0, 0), (0, 256 - cols)))
    first = jnp.concatenate(
        [jnp.broadcast_to(first[None, :, :heads], (Z, X * rows, heads)), resid], axis=2
    )
    first = lax.all_to_all(first, "z", 0, 0, tiled=True).reshape(chunk, heads + 256)

    out_side = shifted(out_near, "y", 1)
    out_near_far, out_side_far = shifted(out_near, "pair", 1), shifted(out_side, "pair", 1)

    gate_t, up_t = after((gate_t, up_t), out_near)
    half = slab // 2
    pieces = []
    for d in range(X):
        begin = (at_x + d) % X * slab + core * half
        pieces.append(
            jnp.concatenate([lanes(gate_t, begin, half), lanes(up_t, begin, half)], axis=0)
        )
    gate_up_near = jnp.concatenate(
        [pieces[0]] + [shifted(pieces[d], "x", d) for d in range(1, X)], axis=0
    )
    gate_up_side = shifted(after(gate_up_near, out_side), "y", 1)
    gate_up_near_far = shifted(gate_up_near, "pair", 1)
    gate_up_side_far = shifted(gate_up_side, "pair", 1)

    down_weight = after(down_weight, out_side)
    half = width // (2 * Y)
    down_side = shifted(
        lanes(down_weight, (1 - at_y) * (width // Y) + core * half, half), "y", 1
    )
    square = jnp.concatenate(
        [lanes(down_weight, at_y * (width // Y) + core * half, half), down_side], axis=0
    )
    square = after(square, gate_up_near)
    down_near = [square] + [shifted(square, "x", d) for d in range(1, X)]

    own, *sends = call(
        project_kernel,
        [jax.ShapeDtypeStruct((cols, chunk), t) for t in (f32, bf16, bf16, bf16)],
        [smem(), vmem()] + [anywhere()] * 4,
        [pltpu.VMEM((X * cols, heads), bf16), pltpu.SemaphoreType.DMA((4,))],
        (2 * X * cols * chunk * heads, X * cols * heads * 4),
    )(at, first, out_near, out_near_far, out_side, out_side_far)
    received = [shifted(send, "x", -d) for d, send in enumerate(sends, 1)]
    second, proj = call(
        norm_kernel,
        [
            jax.ShapeDtypeStruct((Z, cols + 8, chunk), bf16),
            jax.ShapeDtypeStruct((chunk, 256), f32),
        ],
        [vmem()] * 6,
        [],
        (10 * cols * chunk, 20 * cols * chunk),
    )(first, own, *received, gain)
    second = lax.all_to_all(second, "z", 0, 0, tiled=True)

    message = (Z * rows, 2 * span + 256)
    own, *sends = call(
        gate_up_kernel,
        [jax.ShapeDtypeStruct(message, t) for t in (f32, bf16, bf16, bf16)],
        [smem(), vmem(), vmem()] + [anywhere()] * 4,
        [
            pltpu.VMEM((2 * span, slab), bf16),
            pltpu.VMEM((slab, chunk), bf16),
            pltpu.VMEM((chunk, message[1]), f32),
            pltpu.SemaphoreType.DMA((8 * X + Z,)),
        ],
        (4 * span * slab * chunk, 2 * span * slab * 4),
    )(at, second, proj, gate_up_near, gate_up_near_far, gate_up_side, gate_up_side_far)
    received = [shifted(send, "x", e) for e, send in enumerate(sends, 1)]
    down_near = jnp.concatenate(after(down_near, own), axis=0)
    down_far = shifted(down_near, "pair", 1)
    keep, send = call(
        lambda *refs: act_kernel(refs[0], width, *refs[1:]),
        [jax.ShapeDtypeStruct((Z * rows, span + 512), bf16)] * 2,
        [smem()] + [vmem()] * 4,
        [pltpu.VMEM((X, Z * rows, 256), bf16)],
        (20 * span * Z * rows, 20 * span * Z * rows),
    )(at, own, *received)
    other = shifted(send, "y", 1)
    result = call(
        down_kernel,
        jax.ShapeDtypeStruct((Z, Y * rows, width // Y), bf16),
        [smem(), vmem(), vmem()] + [anywhere()] * 2,
        [
            pltpu.VMEM((span, width // Y), bf16),
            pltpu.VMEM((Y * Z * rows, span + 512), bf16),
            pltpu.VMEM((Y * Z * rows, width // Y), f32),
            pltpu.SemaphoreType.DMA((4 * X,)),
        ],
        (2 * span * Y * Z * rows * width // Y, span * width // Y * 4),
    )(at, keep, other, down_near, down_far)
    result = lax.all_to_all(result, "z", 0, 0, tiled=True)
    result = jnp.sum(result.astype(f32), axis=0).reshape(Y, rows, width // Y)
    mine = lax.dynamic_index_in_dim(result, at_y, 0, keepdims=False)
    theirs = lax.dynamic_index_in_dim(result, 1 - at_y, 0, keepdims=False)
    theirs = shifted(theirs, "y", 1)
    result = jnp.where(
        at_y == 0,
        jnp.concatenate([mine, theirs], axis=1),
        jnp.concatenate([theirs, mine], axis=1),
    )
    return (result + hidden_in.astype(f32)).astype(bf16)


def solution(mesh):
    fine = Mesh(mesh.devices.reshape(2, 2, X, Z, Y), ("role", "pair", "x", "z", "y"))
    dev = ("x", "z", "y")
    every = ("role", "pair") + dev
    return jax.shard_map(
        per_device,
        mesh=fine,
        in_specs=(
            P(every, None),
            P(every, None),
            P(every, None),
            P(every, None, None),
            P(every, None),
            P(every),
            P(every, None),
            P(None, dev),
            P(dev),
            P(None, dev),
            P(None, dev),
            P(dev, None),
        ),
        out_specs=P(every, None),
        check_vma=False,
    )
```

```python
import jax
import jax.numpy as jnp
from jax import lax
from jax.experimental import pallas as pl
from jax.experimental.pallas import tpu as pltpu
from jax.sharding import Mesh, PartitionSpec as P

norm_eps = 1e-05
X, Z, Y = 4, 8, 2
LINE = Z * Y
f32, bf16 = jnp.float32, jnp.bfloat16
NT = (((1,), (1,)), ((), ()))
VMEM_LIMIT = 58 * 1024 * 1024


def smem():
    return pl.BlockSpec(memory_space=pltpu.SMEM)


def vmem():
    return pl.BlockSpec(memory_space=pltpu.VMEM)


def anywhere():
    return pl.BlockSpec(memory_space=pl.ANY)


def call(kernel, outs, ins, scratch, cost, out_specs=None):
    if out_specs is None:
        out_specs = [vmem()] * len(outs) if isinstance(outs, (list, tuple)) else vmem()
    return pl.pallas_call(
        kernel,
        out_shape=outs,
        in_specs=ins,
        out_specs=out_specs,
        scratch_shapes=scratch,
        compiler_params=pltpu.CompilerParams(vmem_limit_bytes=VMEM_LIMIT),
        cost_estimate=pl.CostEstimate(flops=cost[0], bytes_accessed=cost[1], transcendentals=0),
    )


def gather_pieces(pieces, sems):
    copies = [
        pltpu.make_async_copy(source, target, sems.at[i]) for i, (source, target) in enumerate(pieces)
    ]
    for copy in copies:
        copy.start()
    return copies


def wait_all(copies):
    for copy in copies:
        copy.wait()


def offset(value, unit):
    return pl.multiple_of(value, unit)


def attend_kernel(
    at, counts, tails, order, q_ref, new_ref, kv_any, gate, up, down,
    out_ref, g0, g1, g2, g3, down_keep, down_send,
    kv_ref, score, top, total, mixed, kv_sems, sems,
):
    core, at_x, at_y = at[0], at[1], at[3]
    rows, heads, size = q_ref.shape
    pool, block, _ = kv_ref.shape
    loads = gather_pieces([(kv_any.at[order[0, p]], kv_ref.at[p]) for p in range(pool)], kv_sems)
    ff, half = gate.shape[0], g0.shape[1]
    pieces = []
    for d, out in ((1, g1), (2, g2), (3, g3), (0, g0)):
        begin = (at_x + d) % X * (2 * half) + core * half
        for part, source in enumerate((gate, up)):
            pieces.append(
                (source.at[:, pl.ds(offset(begin, 128), half)], out.at[pl.ds(part * ff, ff)])
            )
    half = down_keep.shape[1]
    for y, out in ((1 - at_y, down_send), (at_y, down_keep)):
        begin = offset(y * (2 * half) + core * half, 128)
        pieces.append((down.at[:, pl.ds(begin, half)], out))
    slices = gather_pieces(pieces, sems)
    scale = size ** (-0.5)
    owner, limit = [], []
    row, rank = jnp.int32(0), jnp.int32(0)
    for p in range(pool):
        last = rank + 1 == counts[0, row]
        owner.append(row)
        limit.append(jnp.where(last, tails[row], block))
        row = jnp.minimum(jnp.where(last, row + 1, row), rows - 1)
        rank = jnp.where(last, 0, rank + 1)
    own = []
    for r in range(rows):
        key = new_ref[r : r + 1, :size].astype(f32)
        own.append(jnp.sum(q_ref[r].astype(f32) * key, axis=1, keepdims=True) * scale)
        top[r] = jnp.broadcast_to(own[r], (heads, 128))
    lane = lax.broadcasted_iota(jnp.int32, (heads, block), 1)
    for p in range(pool):
        loads[p].wait()
        s = lax.dot_general(q_ref[owner[p]], kv_ref[p, :, :size], NT, preferred_element_type=f32)
        s = jnp.where(lane < limit[p], s * scale, -jnp.inf)
        score[p] = s
        top[owner[p]] = jnp.maximum(top[owner[p]], jnp.max(s, axis=1, keepdims=True))
    for r in range(rows):
        weight = jnp.exp(own[r] - top[r][:, :1])
        total[r] = jnp.broadcast_to(weight, (heads, 128))
        mixed[r] = weight * new_ref[r : r + 1, size:].astype(f32)
    for p in range(pool):
        weight = jnp.exp(score[p] - top[owner[p]][:, :1])
        total[owner[p]] += jnp.sum(weight, axis=1, keepdims=True)
        mixed[owner[p]] += jnp.dot(
            weight.astype(bf16), kv_ref[p, :, size:], preferred_element_type=f32
        )
    for r in range(rows):
        out_ref[r] = (mixed[r] / total[r][:, :1]).astype(bf16)
    wait_all(slices)


def attend(at, queries, new_kv, kv_cache, block_counts, tail_lens, block_order, gate_t, up_t, down):
    rows = queries.shape[0]
    pool, block, twice = kv_cache.shape
    size = twice // 2
    heads = queries.shape[1] // size
    ff, width = gate_t.shape
    piece = jax.ShapeDtypeStruct((2 * ff, width // X // 2), bf16)
    down_piece = jax.ShapeDtypeStruct((ff, width // Y // 2), bf16)
    mixed, *pieces = call(
        attend_kernel,
        [jax.ShapeDtypeStruct((rows, heads, size), bf16)] + [piece] * X + [down_piece] * 2,
        [smem()] * 4 + [vmem()] * 2 + [anywhere()] * 4,
        [
            pltpu.VMEM(kv_cache.shape, bf16),
            pltpu.VMEM((pool, heads, block), f32),
            pltpu.VMEM((rows, heads, 128), f32),
            pltpu.VMEM((rows, heads, 128), f32),
            pltpu.VMEM((rows, heads, size), f32),
            pltpu.SemaphoreType.DMA((pool,)),
            pltpu.SemaphoreType.DMA((2 * X + 2,)),
        ],
        (4 * pool * heads * block * size, pool * block * twice * 2),
        None,
    )(
        at, block_counts, tail_lens, block_order, queries.reshape(rows, heads, size), new_kv,
        kv_cache, gate_t, up_t, down,
    )
    return mixed.reshape(rows, heads * size), pieces[:X], pieces[X:]


def join_kernel(*refs):
    sources, out, sems = refs[:-2], refs[-2], refs[-1]
    pieces, at = [], 0
    for source in sources:
        pieces.append((source, out.at[pl.ds(at, source.shape[0])]))
        at += source.shape[0]
    wait_all(gather_pieces(pieces, sems))


def join(pieces):
    shape = (sum(piece.shape[0] for piece in pieces), pieces[0].shape[1])
    return call(
        join_kernel,
        jax.ShapeDtypeStruct(shape, bf16),
        [anywhere()] * len(pieces),
        [pltpu.SemaphoreType.DMA((len(pieces),))],
        (0, shape[0] * shape[1] * 4),
    )(*pieces)


def project_kernel(
    at, first, near, near_far, side, side_far, own_out, o1, o2, o3, weight, heads, sems
):
    core, at_y = at[0], at[3]
    cols, half = near.shape[0] // X, near.shape[1]
    width = 2 * half
    pieces = [(first.at[:, pl.ds(0, width)], heads)]
    for which, c, y in (
        (near, core, at_y),
        (near_far, 1 - core, at_y),
        (side, core, 1 - at_y),
        (side_far, 1 - core, 1 - at_y),
    ):
        rows = pl.ds(offset(y * X * cols, 16), X * cols)
        pieces.append((which, weight.at[rows, pl.ds(offset(c * half, 128), half)]))
    wait_all(gather_pieces(pieces, sems))
    for y in range(Y):
        got = lax.dot_general(
            weight[y * X * cols : (y + 1) * X * cols], heads[...], NT, preferred_element_type=f32
        )
        for d, out in enumerate((own_out, o1, o2, o3)):
            out[y * cols : (y + 1) * cols] = got[d * cols : (d + 1) * cols].astype(out.dtype)


def norm_kernel(first, own, r1, r2, r3, gain, second, proj_out):
    cols = own.shape[0]
    width = first.shape[1] - 256
    proj = own[...] + r1[...].astype(f32) + r2[...].astype(f32) + r3[...].astype(f32)
    resid = first[:, width:].astype(f32).T
    stream = proj + resid[:cols]
    squares = jnp.sum(stream * stream, axis=0, keepdims=True)
    high = squares.astype(bf16).astype(f32)
    line = lax.broadcasted_iota(jnp.int32, (8, stream.shape[1]), 0)
    tail = jnp.where(line == 0, high, jnp.where(line == 1, squares - high, 0.0)).astype(bf16)
    scaled = (stream * gain[...]).astype(bf16)
    for z in range(Z):
        second[z, :cols] = scaled
        second[z, cols:] = tail
    proj_out[...] = jnp.concatenate(
        [proj, jnp.zeros((256 - cols, proj.shape[1]), f32)], axis=0
    ).T


def gate_up_kernel(
    at, second, proj, near, near_far, side, side_far,
    own_out, o1, o2, o3,
    weight, normed, columns, total, sems,
):
    core, at_x, at_y = at[0], at[1], at[3]
    ff2, half = near.shape[0] // X, near.shape[1]
    ff = ff2 // 2
    span = X * Y * ff
    cols = normed.shape[0] // Z
    pieces = [
        (second.at[z, pl.ds(0, cols)], normed.at[pl.ds(z * cols, cols)]) for z in range(Z)
    ]
    for s, sources in enumerate(((near, near_far), (side, side_far))):
        for d in range(X):
            for which, c in zip(sources, (core, 1 - core)):
                rows = pl.ds((s * X + d) * ff2, ff2)
                pieces.append(
                    (
                        which.at[pl.ds(d * ff2, ff2)],
                        weight.at[rows, pl.ds(offset(c * half, 128), half)],
                    )
                )
    copies = gather_pieces(pieces, sems)
    squares = jnp.sum(second[:, cols : cols + 8].astype(f32), axis=0).T
    squares = squares[:, 0:1] + squares[:, 1:2]
    high = squares.astype(bf16).astype(f32)
    lane = lax.broadcasted_iota(jnp.int32, proj.shape, 1)
    total[:, 2 * span :] = jnp.where(
        lane == cols, high, jnp.where(lane == cols + 1, squares - high, proj[...])
    )
    wait_all(copies[:Z])
    for s in range(Y):
        y = at_y if s == 0 else 1 - at_y
        for d in range(X):
            i = s * X + d
            wait_all(copies[Z + 2 * i : Z + 2 * i + 2])
            got = jnp.dot(
                weight[i * ff2 : (i + 1) * ff2], normed[...], preferred_element_type=f32
            )
            block = (y * X + (at_x + X - d) % X) * ff
            columns[pl.ds(offset(block, 16), ff)] = got[:ff]
            columns[pl.ds(offset(span + block, 16), ff)] = got[ff:]
    step = 384
    for i in range(2 * span // step):
        rows = slice(i * step, (i + 1) * step)
        total[:, rows] = columns[rows].T
    for e, out in enumerate((own_out, o1, o2, o3)):
        to = (at_x + e) % X
        for z in range(0, Z, 2):
            pair = [total[pl.ds(offset(((z + i) * X + to) * 8, 8), 8)] for i in range(2)]
            out[z * 8 : (z + 2) * 8] = jnp.concatenate(pair, axis=0).astype(out.dtype)


def act_kernel(at, width, own, r1, r2, r3, keep, send, shares):
    at_x, at_y = at[1], at[3]
    span = keep.shape[1] - 512
    summed = own[...] + r1[...].astype(f32) + r2[...].astype(f32) + r3[...].astype(f32)
    for e, r in enumerate((own, r1, r2, r3)):
        shares[e] = r[:, 2 * span :].astype(bf16)
    cols = 2 * span + 224
    squares = summed[:, cols : cols + 1] + summed[:, cols + 1 : cols + 2]
    scale = lax.rsqrt(squares / width + norm_eps)
    gate, up = summed[:, :span] * scale, summed[:, span : 2 * span] * scale
    hidden = (gate / (1.0 + jnp.exp(-gate)) * up).astype(bf16)
    for out, y in ((keep, at_y), (send, 1 - at_y)):
        out[:, :span] = hidden
        for j in range(2):
            e = (at_x + X - (2 * y + j)) % X
            out[:, span + j * 256 : span + (j + 1) * 256] = shares[e]


def down_kernel(at, keep, other, near, far, out, weight, act, total, sems):
    core, at_x, at_z, at_y = at[0], at[1], at[2], at[3]
    rows = keep.shape[0]
    half = near.shape[1]
    width = 2 * half
    ff = near.shape[0] // (X * Y)
    span = X * Y * ff
    pieces = []
    for which, c in ((near, core), (far, 1 - core)):
        lanes = pl.ds(offset(c * half, 128), half)
        for d in range(X):
            for side in range(Y):
                y = at_y if side == 0 else 1 - at_y
                block = (y * X + (at_x + X - d) % X) * ff
                pieces.append(
                    (
                        which.at[pl.ds((d * Y + side) * ff, ff)],
                        weight.at[pl.ds(offset(block, 16), ff), lanes],
                    )
                )
    copies = gather_pieces(pieces, sems)
    act[pl.ds(offset(at_y * rows, 16), rows)] = keep[...]
    act[pl.ds(offset((1 - at_y) * rows, 16), rows)] = other[...]
    for i, c in enumerate((core, 1 - core)):
        wait_all(copies[i * X * Y : (i + 1) * X * Y])
        here = pl.ds(offset(c * half, 128), half)
        total[:, here] = jnp.dot(act[:, :span], weight[:, here], preferred_element_type=f32)
    row = lax.broadcasted_iota(jnp.int32, (256, 384), 0)
    lane = lax.broadcasted_iota(jnp.int32, (256, 384), 1)
    for j in range(2):
        spot = j * half + at_z * 224
        base = jnp.minimum(spot // 128 * 128, width - 384)
        pick = jnp.where(row < 224, (row + (spot - base) == lane).astype(f32), 0.0).astype(bf16)
        lanes = pl.ds(offset(base, 128), 384)
        total[:, lanes] += jnp.dot(
            act[:, span + j * 256 : span + (j + 1) * 256], pick, preferred_element_type=f32
        )
    for z in range(Z):
        both = [total[y * rows + z * 8 : y * rows + (z + 1) * 8] for y in range(Y)]
        out[z] = jnp.concatenate(both, axis=0).astype(bf16)


def shifted(value, axis, step):
    size = lax.axis_size(axis)
    return lax.ppermute(value, axis, [(i, (i + step) % size) for i in range(size)])


def after(values, *others):
    return lax.optimization_barrier((values, others))[0]


def lanes(weight, begin, size):
    return lax.dynamic_slice_in_dim(weight, begin, size, 1)


def per_device(
    hidden_in,
    queries,
    new_kv,
    kv_cache,
    block_counts,
    tail_lens,
    block_order,
    out_weight,
    norm_gain,
    gate_weight,
    up_weight,
    down_weight,
):
    core, at_x, at_z, at_y = (lax.axis_index(a) for a in ("pair", "x", "z", "y"))
    at = jnp.stack([core, at_x, at_z, at_y])
    rows, width = hidden_in.shape
    slab = width // X
    block = width // (X * Z * Y)
    cols = Y * block
    chunk = X * Z * rows
    ff = gate_weight.shape[1]
    span = X * Y * ff
    heads = queries.shape[1] // X
    out_t, gate_t, up_t = out_weight.T, gate_weight.T, up_weight.T

    half = heads // 2
    pieces = [lanes(out_t, (at_x + d) % X * heads + core * half, half) for d in range(X)]
    out_near = join([pieces[0]] + [shifted(pieces[d], "x", d) for d in range(1, X)])
    gain = shifted(norm_gain, "y", 1)
    gain = jnp.where(
        at_y == 0, jnp.concatenate([norm_gain, gain]), jnp.concatenate([gain, norm_gain])
    )[:, None]

    attended, gate_up_pieces, down_pieces = attend(
        at, queries, new_kv, kv_cache, block_counts, tail_lens, block_order, gate_t, up_t, down_weight
    )
    first = jnp.concatenate(
        [attended.reshape(rows, X, heads), hidden_in.reshape(rows, X, slab)], axis=2
    ).transpose(1, 0, 2)
    first = after(first, (out_near, gain))
    first = lax.all_to_all(first, "x", 0, 0, tiled=True).reshape(X * rows, heads + slab)
    resid = first[:, heads:].reshape(X * rows, Z, cols).transpose(1, 0, 2)
    resid = jnp.pad(resid, ((0, 0), (0, 0), (0, 256 - cols)))
    first = jnp.concatenate(
        [jnp.broadcast_to(first[None, :, :heads], (Z, X * rows, heads)), resid], axis=2
    )
    ready = first
    first = lax.all_to_all(first, "z", 0, 0, tiled=True).reshape(chunk, heads + 256)

    out_side = shifted(out_near, "y", 1)
    out_near_far, out_side_far = shifted(out_near, "pair", 1), shifted(out_side, "pair", 1)

    down_side = shifted(after(down_pieces[1], out_near), "y", 1)

    pieces = after(gate_up_pieces, out_near)
    gate_up_near = after([shifted(pieces[d], "x", d) for d in range(1, X)], ready)
    gate_up_near = join([pieces[0]] + gate_up_near)
    gate_up_side = shifted(after(gate_up_near, (out_side, down_side)), "y", 1)
    square = join([after(down_pieces[0], gate_up_near), down_side])
    down_near = [square, shifted(square, "x", 1), shifted(square, "x", -1)]

    own, *sends = call(
        project_kernel,
        [jax.ShapeDtypeStruct((cols, chunk), t) for t in (f32, bf16, bf16, bf16)],
        [smem()] + [anywhere()] * 5,
        [
            pltpu.VMEM((X * cols, heads), bf16),
            pltpu.VMEM((chunk, heads), bf16),
            pltpu.SemaphoreType.DMA((5,)),
        ],
        (2 * X * cols * chunk * heads, X * cols * heads * 4),
    )(at, first, out_near, out_near_far, out_side, out_side_far)
    received = [shifted(send, "x", -d) for d, send in enumerate(sends, 1)]
    received = after(received, down_near)
    second, proj = call(
        norm_kernel,
        [
            jax.ShapeDtypeStruct((Z, cols + 8, chunk), bf16),
            jax.ShapeDtypeStruct((chunk, 256), f32),
        ],
        [vmem()] * 6,
        [],
        (10 * cols * chunk, 20 * cols * chunk),
    )(first, own, *received, gain)
    gate_up_near, gate_up_side, square = after((gate_up_near, gate_up_side, square), second)
    gate_up_near_far = shifted(gate_up_near, "pair", 1)
    gate_up_side_far = shifted(gate_up_side, "pair", 1)
    down_across = shifted(square, "x", 2)
    second = lax.all_to_all(second, "z", 0, 0, tiled=True)

    message = (Z * rows, 2 * span + 256)
    own, *sends = call(
        gate_up_kernel,
        [jax.ShapeDtypeStruct(message, t) for t in (f32, bf16, bf16, bf16)],
        [smem(), vmem(), vmem()] + [anywhere()] * 4,
        [
            pltpu.VMEM((2 * span, slab), bf16),
            pltpu.VMEM((slab, chunk), bf16),
            pltpu.VMEM((2 * span, chunk), f32),
            pltpu.VMEM((chunk, message[1]), f32),
            pltpu.SemaphoreType.DMA((4 * X + Z,)),
        ],
        (4 * span * slab * chunk, 2 * span * slab * 4),
    )(at, second, proj, gate_up_near, gate_up_near_far, gate_up_side, gate_up_side_far)
    received = [shifted(send, "x", e) for e, send in enumerate(sends, 1)]
    down_across = after(down_across, received)
    down_near = join([down_near[0], down_near[1], down_across, down_near[2]])
    down_far = shifted(down_near, "pair", 1)
    keep, send = call(
        lambda *refs: act_kernel(refs[0], width, *refs[1:]),
        [jax.ShapeDtypeStruct((Z * rows, span + 512), bf16)] * 2,
        [smem()] + [vmem()] * 4,
        [pltpu.VMEM((X, Z * rows, 256), bf16)],
        (20 * span * Z * rows, 20 * span * Z * rows),
    )(at, own, *received)
    other = shifted(send, "y", 1)
    result = call(
        down_kernel,
        jax.ShapeDtypeStruct((Z, Y * rows, width // Y), bf16),
        [smem(), vmem(), vmem()] + [anywhere()] * 2,
        [
            pltpu.VMEM((span, width // Y), bf16),
            pltpu.VMEM((Y * Z * rows, span + 512), bf16),
            pltpu.VMEM((Y * Z * rows, width // Y), f32),
            pltpu.SemaphoreType.DMA((4 * X,)),
        ],
        (2 * span * Y * Z * rows * width // Y, span * width // Y * 4),
    )(at, keep, other, down_near, down_far)
    result = lax.all_to_all(result, "z", 0, 0, tiled=True)
    result = jnp.sum(result.astype(f32), axis=0).reshape(Y, rows, width // Y)
    mine = lax.dynamic_index_in_dim(result, at_y, 0, keepdims=False)
    theirs = lax.dynamic_index_in_dim(result, 1 - at_y, 0, keepdims=False)
    theirs = shifted(theirs, "y", 1)
    result = jnp.where(
        at_y == 0,
        jnp.concatenate([mine, theirs], axis=1),
        jnp.concatenate([theirs, mine], axis=1),
    )
    return (result + hidden_in.astype(f32)).astype(bf16)


def solution(mesh):
    fine = Mesh(mesh.devices.reshape(2, 2, X, Z, Y), ("role", "pair", "x", "z", "y"))
    dev = ("x", "z", "y")
    every = ("role", "pair") + dev
    return jax.shard_map(
        per_device,
        mesh=fine,
        in_specs=(
            P(every, None),
            P(every, None),
            P(every, None),
            P(every, None, None),
            P(every, None),
            P(every),
            P(every, None),
            P(None, dev),
            P(dev),
            P(None, dev),
            P(None, dev),
            P(dev, None),
        ),
        out_specs=P(every, None),
        check_vma=False,
    )
```

```python
import jax
import jax.numpy as jnp
from jax import lax
from jax.experimental import pallas as pl
from jax.experimental.pallas import tpu as pltpu
from jax.sharding import Mesh, PartitionSpec as P

norm_eps = 1e-05
X, Z, Y = 4, 8, 2
LINE = Z * Y
f32, bf16 = jnp.float32, jnp.bfloat16
NT = (((1,), (1,)), ((), ()))
MIB = 1024 * 1024


def smem():
    return pl.BlockSpec(memory_space=pltpu.SMEM)


def vmem():
    return pl.BlockSpec(memory_space=pltpu.VMEM)


def anywhere():
    return pl.BlockSpec(memory_space=pl.ANY)


def call(kernel, outs, ins, scratch, cost, mib):
    single = not isinstance(outs, (list, tuple))
    return pl.pallas_call(
        kernel,
        out_shape=outs,
        in_specs=ins,
        out_specs=vmem() if single else [vmem()] * len(outs),
        scratch_shapes=scratch,
        compiler_params=pltpu.CompilerParams(vmem_limit_bytes=mib * MIB),
        cost_estimate=pl.CostEstimate(flops=cost[0], bytes_accessed=cost[1], transcendentals=0),
    )


def gather_pieces(pieces, sems):
    copies = [
        pltpu.make_async_copy(source, target, sems.at[i]) for i, (source, target) in enumerate(pieces)
    ]
    for copy in copies:
        copy.start()
    return copies


def wait_all(copies):
    for copy in copies:
        copy.wait()


def offset(value, unit):
    return pl.multiple_of(value, unit)


def cut_kernel(at, gate, up, down, p0, p1, p2, p3, sems):
    core, at_x = at[0], at[1]
    ff, half = gate.shape[0], p0.shape[1]
    pieces = []
    for d, out in ((1, p1), (3, p3), (2, p2), (0, p0)):
        begin = offset((at_x + d) % X * (2 * half) + core * half, 128)
        for part, source in enumerate((gate, up, down)):
            pieces.append((source.at[:, pl.ds(begin, half)], out.at[pl.ds(part * ff, ff)]))
    wait_all(gather_pieces(pieces, sems))


def cut(at, gate_t, up_t, down):
    ff, width = gate_t.shape
    return call(
        cut_kernel,
        [jax.ShapeDtypeStruct((3 * ff, width // X // 2), bf16)] * X,
        [smem()] + [anywhere()] * 3,
        [pltpu.SemaphoreType.DMA((3 * X,))],
        (0, 6 * ff * width),
        58,
    )(at, gate_t, up_t, down)


def attend_kernel(
    counts, tails, order, q_ref, new_ref, kv_ref, out_ref, score, top, total, mixed
):
    rows, heads, size = q_ref.shape
    pool, block, _ = kv_ref.shape
    scale = size ** (-0.5)
    owner, limit = [], []
    row, rank = jnp.int32(0), jnp.int32(0)
    for p in range(pool):
        last = rank + 1 == counts[0, row]
        owner.append(row)
        limit.append(jnp.where(last, tails[row], block))
        row = jnp.minimum(jnp.where(last, row + 1, row), rows - 1)
        rank = jnp.where(last, 0, rank + 1)
    own = []
    for r in range(rows):
        key = new_ref[r : r + 1, :size].astype(f32)
        own.append(jnp.sum(q_ref[r].astype(f32) * key, axis=1, keepdims=True) * scale)
        top[r] = jnp.broadcast_to(own[r], (heads, 128))
    lane = lax.broadcasted_iota(jnp.int32, (heads, block), 1)
    for p in range(pool):
        s = lax.dot_general(
            q_ref[owner[p]], kv_ref[order[0, p], :, :size], NT, preferred_element_type=f32
        )
        s = jnp.where(lane < limit[p], s * scale, -jnp.inf)
        score[p] = s
        top[owner[p]] = jnp.maximum(top[owner[p]], jnp.max(s, axis=1, keepdims=True))
    for r in range(rows):
        weight = jnp.exp(own[r] - top[r][:, :1])
        total[r] = jnp.broadcast_to(weight, (heads, 128))
        mixed[r] = weight * new_ref[r : r + 1, size:].astype(f32)
    for p in range(pool):
        weight = jnp.exp(score[p] - top[owner[p]][:, :1])
        total[owner[p]] += jnp.sum(weight, axis=1, keepdims=True)
        mixed[owner[p]] += jnp.dot(
            weight.astype(bf16), kv_ref[order[0, p], :, size:], preferred_element_type=f32
        )
    for r in range(rows):
        out_ref[r] = (mixed[r] / total[r][:, :1]).astype(bf16)


def attend(queries, new_kv, kv_cache, block_counts, tail_lens, block_order):
    rows = queries.shape[0]
    pool, block, twice = kv_cache.shape
    size = twice // 2
    heads = queries.shape[1] // size
    mixed = call(
        attend_kernel,
        jax.ShapeDtypeStruct((rows, heads, size), bf16),
        [smem()] * 3 + [vmem()] * 3,
        [
            pltpu.VMEM((pool, heads, block), f32),
            pltpu.VMEM((rows, heads, 128), f32),
            pltpu.VMEM((rows, heads, 128), f32),
            pltpu.VMEM((rows, heads, size), f32),
        ],
        (4 * pool * heads * block * size, pool * block * twice * 2),
        58,
    )(block_counts, tail_lens, block_order, queries.reshape(rows, heads, size), new_kv, kv_cache)
    return mixed.reshape(rows, heads * size)


def join_kernel(*refs):
    sources, out, sems = refs[:-2], refs[-2], refs[-1]
    pieces, row = [], 0
    for source in sources:
        pieces.append((source, out.at[pl.ds(row, source.shape[0])]))
        row += source.shape[0]
    wait_all(gather_pieces(pieces, sems))


def join(pieces):
    shape = (sum(piece.shape[0] for piece in pieces), pieces[0].shape[1])
    return call(
        join_kernel,
        jax.ShapeDtypeStruct(shape, bf16),
        [anywhere()] * len(pieces),
        [pltpu.SemaphoreType.DMA((len(pieces),))],
        (0, shape[0] * shape[1] * 4),
        58,
    )(*pieces)


def project_kernel(
    at, first, near, near_far, side, side_far, own_out, o1, o2, o3, weight, heads, sems
):
    core, at_y = at[0], at[3]
    cols, half = near.shape[0] // X, near.shape[1]
    width = 2 * half
    pieces = [(first.at[:, pl.ds(0, width)], heads)]
    for which, c, y in (
        (near, core, at_y),
        (side, core, 1 - at_y),
        (near_far, 1 - core, at_y),
        (side_far, 1 - core, 1 - at_y),
    ):
        rows = pl.ds(offset(y * X * cols, 16), X * cols)
        pieces.append((which, weight.at[rows, pl.ds(offset(c * half, 128), half)]))
    wait_all(gather_pieces(pieces, sems))
    for y in range(Y):
        got = lax.dot_general(
            weight[y * X * cols : (y + 1) * X * cols], heads[...], NT, preferred_element_type=f32
        )
        for d, out in enumerate((own_out, o1, o2, o3)):
            out[y * cols : (y + 1) * cols] = got[d * cols : (d + 1) * cols].astype(out.dtype)


def norm_kernel(first, own, r1, r2, r3, gain, second, proj_out):
    cols = own.shape[0]
    width = first.shape[1] - 256
    proj = own[...] + r1[...].astype(f32) + r2[...].astype(f32) + r3[...].astype(f32)
    resid = first[:, width:].astype(f32).T
    stream = proj + resid[:cols]
    squares = jnp.sum(stream * stream, axis=0, keepdims=True)
    high = squares.astype(bf16).astype(f32)
    line = lax.broadcasted_iota(jnp.int32, (8, stream.shape[1]), 0)
    tail = jnp.where(line == 0, high, jnp.where(line == 1, squares - high, 0.0)).astype(bf16)
    scaled = (stream * gain[...]).astype(bf16)
    for z in range(Z):
        second[z, :cols] = scaled
        second[z, cols:] = tail
    proj_out[...] = jnp.concatenate(
        [proj, jnp.zeros((256 - cols, proj.shape[1]), f32)], axis=0
    ).T


def sources_of(at, own, far):
    return [(which, c) for a, b in zip(own, far) for which, c in ((a, at[0]), (b, 1 - at[0]))]


def gate_up_kernel(
    at, second, w0, w1, w2, w3, f0, f1, f2, f3,
    own_out, o1, o2, o3, weight, normed, columns, total, sems,
):
    at_x, at_y = at[1], at[3]
    both, half = X // 2, w0.shape[1]
    ff = w0.shape[0] // (3 * both)
    ff2 = 2 * ff
    span = X * Y * ff
    cols = normed.shape[0] // Z
    pieces = [
        (second.at[z, pl.ds(0, cols)], normed.at[pl.ds(z * cols, cols)]) for z in range(Z)
    ]
    for i, (which, c) in enumerate(sources_of(at, (w0, w1, w2, w3), (f0, f1, f2, f3))):
        lanes = pl.ds(offset(c * half, 128), half)
        for j in range(both):
            rows = pl.ds((i // 2 * both + j) * ff2, ff2)
            pieces.append((which.at[pl.ds(j * 3 * ff, ff2)], weight.at[rows, lanes]))
    copies = gather_pieces(pieces, sems)
    squares = jnp.sum(second[:, cols : cols + 8].astype(f32), axis=0).T
    squares = squares[:, 0:1] + squares[:, 1:2]
    high = squares.astype(bf16).astype(f32)
    lane = lax.broadcasted_iota(jnp.int32, (squares.shape[0], 128), 1)
    total[:, 2 * span :] = jnp.where(
        lane == 0, high, jnp.where(lane == 1, squares - high, 0.0)
    )
    wait_all(copies[:Z])
    for s in range(Y):
        y = at_y if s == 0 else 1 - at_y
        for d in range(X):
            i = s * X + d
            if i % both == 0:
                wait_all(copies[Z + 2 * i : Z + 2 * (i + both)])
            got = jnp.dot(
                weight[i * ff2 : (i + 1) * ff2], normed[...], preferred_element_type=f32
            )
            block = (y * X + (at_x + X - d) % X) * ff
            columns[pl.ds(offset(block, 16), ff)] = got[:ff]
            columns[pl.ds(offset(span + block, 16), ff)] = got[ff:]
    step = 384
    for i in range(2 * span // step):
        rows = slice(i * step, (i + 1) * step)
        total[:, rows] = columns[rows].T
    for e, out in enumerate((own_out, o1, o2, o3)):
        to = (at_x + e) % X
        for z in range(0, Z, 2):
            pair = [total[pl.ds(offset(((z + i) * X + to) * 8, 8), 8)] for i in range(2)]
            out[z * 8 : (z + 2) * 8] = jnp.concatenate(pair, axis=0).astype(out.dtype)


def act_kernel(width, own, r1, r2, r3, hidden):
    span = hidden.shape[1]
    summed = own[...] + r1[...].astype(f32) + r2[...].astype(f32) + r3[...].astype(f32)
    squares = summed[:, 2 * span : 2 * span + 1] + summed[:, 2 * span + 1 : 2 * span + 2]
    scale = lax.rsqrt(squares / width + norm_eps)
    gate, up = summed[:, :span] * scale, summed[:, span : 2 * span] * scale
    hidden[...] = (gate / (1.0 + jnp.exp(-gate)) * up).astype(bf16)


def down_kernel(
    at, h0, h1, h2, h3, proj, w0, w1, w2, w3, f0, f1, f2, f3, out, weight, act, total, sems
):
    at_x, at_z, at_y = at[1], at[2], at[3]
    both, half = X // 2, w0.shape[1]
    width = 2 * half
    ff = w0.shape[0] // (3 * both)
    rows = h0.shape[0]
    pieces = []
    for i, (which, c) in enumerate(sources_of(at, (w0, w1, w2, w3), (f0, f1, f2, f3))):
        lanes = pl.ds(offset(c * half, 128), half)
        y = at_y if i // 4 == 0 else 1 - at_y
        for j in range(both):
            d = i // 2 % 2 * both + j
            block = (y * X + (at_x + X - d) % X) * ff
            pieces.append(
                (
                    which.at[pl.ds((3 * j + 2) * ff, ff)],
                    weight.at[pl.ds(offset(block, 16), ff), lanes],
                )
            )
    copies = gather_pieces(pieces, sems)
    for e, h in enumerate((h0, h1, h2, h3)):
        act[pl.ds(offset((at_x + X - e) % X * rows, 16), rows)] = h[...]
    spot = at_z * 224
    base = jnp.minimum(spot // 128 * 128, width - 384)
    row = lax.broadcasted_iota(jnp.int32, (256, 384), 0)
    lane = lax.broadcasted_iota(jnp.int32, (256, 384), 1)
    pick = jnp.where(row < 224, (row + (spot - base) == lane).astype(f32), 0.0).astype(bf16)
    placed = jnp.dot(proj[...].astype(bf16), pick, preferred_element_type=f32)
    wait_all(copies)
    got = jnp.dot(act[...], weight[...], preferred_element_type=f32)
    for z in range(Z):
        for x in range(X):
            at_row = x * rows + z * 8
            total[(z * X + x) * 8 : (z * X + x + 1) * 8] = got[at_row : at_row + 8]
    total[:, pl.ds(offset(base, 128), 384)] += placed
    out[...] = total[...].astype(bf16).reshape(out.shape)


def shifted(value, axis, step):
    size = lax.axis_size(axis)
    return lax.ppermute(value, axis, [(i, (i + step) % size) for i in range(size)])


def around(low, high):
    size = lax.axis_size("role") * Y
    up = [(i, (i + 1) % size) for i in range(size)]
    return (
        lax.ppermute(low, ("role", "y"), up),
        lax.ppermute(high, ("role", "y"), [(b, a) for a, b in up]),
    )


def pair(values):
    return [shifted(value, "pair", 1) for value in values]


def after(values, *others):
    return lax.optimization_barrier((values, others))[0]


def lanes(weight, begin, size):
    return lax.dynamic_slice_in_dim(weight, begin, size, 1)


def per_device(
    hidden_in,
    queries,
    new_kv,
    kv_cache,
    block_counts,
    tail_lens,
    block_order,
    out_weight,
    norm_gain,
    gate_weight,
    up_weight,
    down_weight,
):
    core, at_x, at_z, at_y = (lax.axis_index(a) for a in ("pair", "x", "z", "y"))
    at = jnp.stack([core, at_x, at_z, at_y])
    rows, width = hidden_in.shape
    slab = width // X
    block = width // (X * Z * Y)
    cols = Y * block
    chunk = X * Z * rows
    ff = gate_weight.shape[1]
    span = X * Y * ff
    heads = queries.shape[1] // X
    out_t, gate_t, up_t = out_weight.T, gate_weight.T, up_weight.T

    half = heads // 2
    pieces = [lanes(out_t, (at_x + d) % X * heads + core * half, half) for d in range(X)]
    out_pieces = [pieces[0]] + [shifted(pieces[d], "x", d) for d in range(1, X)]
    gain = shifted(norm_gain, "y", 1)
    gain = jnp.where(
        at_y == 0, jnp.concatenate([norm_gain, gain]), jnp.concatenate([gain, norm_gain])
    )[:, None]

    attended = attend(queries, new_kv, kv_cache, block_counts, tail_lens, block_order)
    first = jnp.concatenate(
        [attended.reshape(rows, X, heads), hidden_in.reshape(rows, X, slab)], axis=2
    ).transpose(1, 0, 2)
    first = after(first, (out_pieces, gain))
    pieces = cut(at, *after((gate_t, up_t, down_weight), first))
    first = lax.all_to_all(first, "x", 0, 0, tiled=True).reshape(X * rows, heads + slab)
    resid = first[:, heads:].reshape(X * rows, Z, cols).transpose(1, 0, 2)
    resid = jnp.pad(resid, ((0, 0), (0, 0), (0, 256 - cols)))
    first = jnp.concatenate(
        [jnp.broadcast_to(first[None, :, :heads], (Z, X * rows, heads)), resid], axis=2
    )
    first = lax.all_to_all(first, "z", 0, 0, tiled=True).reshape(chunk, heads + 256)

    out_near = join(out_pieces)
    out_side = shifted(out_near, "y", 1)
    out_all = [out_near, *pair([out_near]), out_side, *pair([out_side])]
    moved = [shifted(pieces[1], "x", 1), shifted(pieces[3], "x", -1)]
    across = shifted(after(pieces[2], moved), "x", 2)

    own, *sends = call(
        project_kernel,
        [jax.ShapeDtypeStruct((cols, chunk), t) for t in (f32, bf16, bf16, bf16)],
        [smem()] + [anywhere()] * 5,
        [
            pltpu.VMEM((X * cols, heads), bf16),
            pltpu.VMEM((chunk, heads), bf16),
            pltpu.SemaphoreType.DMA((5,)),
        ],
        (2 * X * cols * chunk * heads, X * cols * heads * 4),
        58,
    )(at, first, *out_all)
    received = [shifted(send, "x", -d) for d, send in enumerate(sends, 1)]
    weights = [join([pieces[0], moved[0]]), join([after(across, own), moved[1]])]
    weights += around(*weights)
    second, proj = call(
        norm_kernel,
        [
            jax.ShapeDtypeStruct((Z, cols + 8, chunk), bf16),
            jax.ShapeDtypeStruct((chunk, 256), f32),
        ],
        [vmem()] * 6,
        [],
        (10 * cols * chunk, 20 * cols * chunk),
        58,
    )(first, own, *received, gain)
    weights = after(weights, second)
    weights += pair(weights)
    second = lax.all_to_all(second, "z", 0, 0, tiled=True)

    message = (Z * rows, 2 * span + 128)
    own, *sends = call(
        gate_up_kernel,
        [jax.ShapeDtypeStruct(message, t) for t in (f32, bf16, bf16, bf16)],
        [smem(), vmem()] + [anywhere()] * 8,
        [
            pltpu.VMEM((2 * span, slab), bf16),
            pltpu.VMEM((slab, chunk), bf16),
            pltpu.VMEM((2 * span, chunk), f32),
            pltpu.VMEM((chunk, message[1]), f32),
            pltpu.SemaphoreType.DMA((16 + Z,)),
        ],
        (4 * span * slab * chunk, 2 * span * slab * 4),
        58,
    )(at, second, *weights)
    received = [shifted(send, "x", e) for e, send in enumerate(sends, 1)]
    hidden = call(
        lambda *refs: act_kernel(width, *refs),
        jax.ShapeDtypeStruct((Z * rows, span), bf16),
        [vmem()] * 4,
        [],
        (20 * span * Z * rows, 20 * span * Z * rows),
        8,
    )(own, *received)
    hidden = [hidden] + [shifted(hidden, "x", e) for e in range(1, X)]
    result = call(
        down_kernel,
        jax.ShapeDtypeStruct((Z, X * rows, slab), bf16),
        [smem()] + [vmem()] * 5 + [anywhere()] * 8,
        [
            pltpu.VMEM((span, slab), bf16),
            pltpu.VMEM((chunk, span), bf16),
            pltpu.VMEM((chunk, slab), f32),
            pltpu.SemaphoreType.DMA((16,)),
        ],
        (2 * span * chunk * slab, span * slab * 4),
        58,
    )(at, *hidden, proj, *weights)
    result = lax.all_to_all(result, "z", 0, 0, tiled=True)
    result = jnp.sum(result.astype(f32), axis=0).reshape(X, rows, slab)
    result = lax.all_to_all(result, "x", 0, 0, tiled=True)
    result = result.transpose(1, 0, 2).reshape(rows, width)
    return (result + hidden_in.astype(f32)).astype(bf16)


def solution(mesh):
    fine = Mesh(mesh.devices.reshape(2, 2, X, Z, Y), ("role", "pair", "x", "z", "y"))
    dev = ("x", "z", "y")
    every = ("role", "pair") + dev
    return jax.shard_map(
        per_device,
        mesh=fine,
        in_specs=(
            P(every, None),
            P(every, None),
            P(every, None),
            P(every, None, None),
            P(every, None),
            P(every),
            P(every, None),
            P(None, dev),
            P(dev),
            P(None, dev),
            P(None, dev),
            P(dev, None),
        ),
        out_specs=P(every, None),
        check_vma=False,
    )
```

```python
import jax
import jax.numpy as jnp
from jax import lax
from jax.experimental import pallas as pl
from jax.experimental.pallas import tpu as pltpu
from jax.sharding import Mesh, PartitionSpec as P

norm_eps = 1e-05
X, Z, Y = 4, 8, 2
LINE = Z * Y
f32, bf16 = jnp.float32, jnp.bfloat16
NT = (((1,), (1,)), ((), ()))
MIB = 1024 * 1024


def smem():
    return pl.BlockSpec(memory_space=pltpu.SMEM)


def vmem():
    return pl.BlockSpec(memory_space=pltpu.VMEM)


def anywhere():
    return pl.BlockSpec(memory_space=pl.ANY)


def call(kernel, outs, ins, scratch, cost, mib):
    single = not isinstance(outs, (list, tuple))
    return pl.pallas_call(
        kernel,
        out_shape=outs,
        in_specs=ins,
        out_specs=vmem() if single else [vmem()] * len(outs),
        scratch_shapes=scratch,
        compiler_params=pltpu.CompilerParams(vmem_limit_bytes=mib * MIB),
        cost_estimate=pl.CostEstimate(flops=cost[0], bytes_accessed=cost[1], transcendentals=0),
    )


def gather_pieces(pieces, sems):
    copies = [
        pltpu.make_async_copy(source, target, sems.at[i]) for i, (source, target) in enumerate(pieces)
    ]
    for copy in copies:
        copy.start()
    return copies


def wait_all(copies):
    for copy in copies:
        copy.wait()


def offset(value, unit):
    return pl.multiple_of(value, unit)


def cut_kernel(at, gate, up, down, p0, p1, p2, p3, sems):
    core, at_x = at[0], at[1]
    ff, half = gate.shape[0], p0.shape[1]
    pieces = []
    for d, out in ((1, p1), (3, p3), (2, p2), (0, p0)):
        begin = offset((at_x + d) % X * (2 * half) + core * half, 128)
        for part, source in enumerate((gate, up, down)):
            pieces.append((source.at[:, pl.ds(begin, half)], out.at[pl.ds(part * ff, ff)]))
    wait_all(gather_pieces(pieces, sems))


def cut(at, gate_t, up_t, down):
    ff, width = gate_t.shape
    return call(
        cut_kernel,
        [jax.ShapeDtypeStruct((3 * ff, width // X // 2), bf16)] * X,
        [smem()] + [anywhere()] * 3,
        [pltpu.SemaphoreType.DMA((3 * X,))],
        (0, 6 * ff * width),
        58,
    )(at, gate_t, up_t, down)


def attend_kernel(
    counts, tails, order, q_ref, new_ref, kv_ref, out_ref, score, top, total, mixed
):
    rows, heads, size = q_ref.shape
    pool, block, _ = kv_ref.shape
    scale = size ** (-0.5)
    owner, limit = [], []
    row, rank = jnp.int32(0), jnp.int32(0)
    for p in range(pool):
        last = rank + 1 == counts[0, row]
        owner.append(row)
        limit.append(jnp.where(last, tails[row], block))
        row = jnp.minimum(jnp.where(last, row + 1, row), rows - 1)
        rank = jnp.where(last, 0, rank + 1)
    own = []
    for r in range(rows):
        key = new_ref[r : r + 1, :size].astype(f32)
        own.append(jnp.sum(q_ref[r].astype(f32) * key, axis=1, keepdims=True) * scale)
        top[r] = jnp.broadcast_to(own[r], (heads, 128))
    lane = lax.broadcasted_iota(jnp.int32, (heads, block), 1)
    for p in range(pool):
        s = lax.dot_general(
            q_ref[owner[p]], kv_ref[order[0, p], :, :size], NT, preferred_element_type=f32
        )
        s = jnp.where(lane < limit[p], s * scale, -jnp.inf)
        score[p] = s
        top[owner[p]] = jnp.maximum(top[owner[p]], jnp.max(s, axis=1, keepdims=True))
    for r in range(rows):
        weight = jnp.exp(own[r] - top[r][:, :1])
        total[r] = jnp.broadcast_to(weight, (heads, 128))
        mixed[r] = weight * new_ref[r : r + 1, size:].astype(f32)
    for p in range(pool):
        weight = jnp.exp(score[p] - top[owner[p]][:, :1])
        total[owner[p]] += jnp.sum(weight, axis=1, keepdims=True)
        mixed[owner[p]] += jnp.dot(
            weight.astype(bf16), kv_ref[order[0, p], :, size:], preferred_element_type=f32
        )
    for r in range(rows):
        out_ref[r] = (mixed[r] / total[r][:, :1]).astype(bf16)


def attend(queries, new_kv, kv_cache, block_counts, tail_lens, block_order):
    rows = queries.shape[0]
    pool, block, twice = kv_cache.shape
    size = twice // 2
    heads = queries.shape[1] // size
    mixed = call(
        attend_kernel,
        jax.ShapeDtypeStruct((rows, heads, size), bf16),
        [smem()] * 3 + [vmem()] * 3,
        [
            pltpu.VMEM((pool, heads, block), f32),
            pltpu.VMEM((rows, heads, 128), f32),
            pltpu.VMEM((rows, heads, 128), f32),
            pltpu.VMEM((rows, heads, size), f32),
        ],
        (4 * pool * heads * block * size, pool * block * twice * 2),
        58,
    )(block_counts, tail_lens, block_order, queries.reshape(rows, heads, size), new_kv, kv_cache)
    return mixed.reshape(rows, heads * size)


def join_kernel(*refs):
    sources, out, sems = refs[:-2], refs[-2], refs[-1]
    pieces, row = [], 0
    for source in sources:
        pieces.append((source, out.at[pl.ds(row, source.shape[0])]))
        row += source.shape[0]
    wait_all(gather_pieces(pieces, sems))


def join(pieces):
    shape = (sum(piece.shape[0] for piece in pieces), pieces[0].shape[1])
    return call(
        join_kernel,
        jax.ShapeDtypeStruct(shape, bf16),
        [anywhere()] * len(pieces),
        [pltpu.SemaphoreType.DMA((len(pieces),))],
        (0, shape[0] * shape[1] * 4),
        58,
    )(*pieces)


def project_kernel(
    at, first, near, near_far, side, side_far, own_out, o1, o2, o3, weight, heads, sems
):
    core, at_y = at[0], at[3]
    cols, half = near.shape[0] // X, near.shape[1]
    width = 2 * half
    pieces = [(first.at[:, pl.ds(0, width)], heads)]
    for which, c, y in (
        (near, core, at_y),
        (side, core, 1 - at_y),
        (near_far, 1 - core, at_y),
        (side_far, 1 - core, 1 - at_y),
    ):
        rows = pl.ds(offset(y * X * cols, 16), X * cols)
        pieces.append((which, weight.at[rows, pl.ds(offset(c * half, 128), half)]))
    wait_all(gather_pieces(pieces, sems))
    for y in range(Y):
        got = lax.dot_general(
            weight[y * X * cols : (y + 1) * X * cols], heads[...], NT, preferred_element_type=f32
        )
        for d, out in enumerate((own_out, o1, o2, o3)):
            out[y * cols : (y + 1) * cols] = got[d * cols : (d + 1) * cols].astype(out.dtype)


def norm_kernel(first, own, r1, r2, r3, gain, second, proj_out):
    cols = own.shape[0]
    width = first.shape[1] - 256
    proj = own[...] + r1[...].astype(f32) + r2[...].astype(f32) + r3[...].astype(f32)
    resid = first[:, width:].astype(f32).T
    stream = proj + resid[:cols]
    squares = jnp.sum(stream * stream, axis=0, keepdims=True)
    high = squares.astype(bf16).astype(f32)
    line = lax.broadcasted_iota(jnp.int32, (8, stream.shape[1]), 0)
    tail = jnp.where(line == 0, high, jnp.where(line == 1, squares - high, 0.0)).astype(bf16)
    scaled = (stream * gain[...]).astype(bf16)
    for z in range(Z):
        second[z, :cols] = scaled
        second[z, cols:] = tail
    proj_out[...] = jnp.concatenate(
        [proj, jnp.zeros((256 - cols, proj.shape[1]), f32)], axis=0
    ).T


def sources_of(at, own, far):
    return [(which, c) for a, b in zip(own, far) for which, c in ((a, at[0]), (b, 1 - at[0]))]


def gate_up_kernel(
    at, second, w0, w1, w2, w3, f0, f1, f2, f3,
    own_out, o1, o2, o3, weight, normed, columns, total, sems,
):
    at_x, at_y = at[1], at[3]
    both, half = X // 2, w0.shape[1]
    ff = w0.shape[0] // (3 * both)
    ff2 = 2 * ff
    span = X * Y * ff
    cols = normed.shape[0] // Z
    pieces = [
        (second.at[z, pl.ds(0, cols)], normed.at[pl.ds(z * cols, cols)]) for z in range(Z)
    ]
    for i, (which, c) in enumerate(sources_of(at, (w0, w1, w2, w3), (f0, f1, f2, f3))):
        lanes = pl.ds(offset(c * half, 128), half)
        for j in range(both):
            rows = pl.ds((i // 2 * both + j) * ff2, ff2)
            pieces.append((which.at[pl.ds(j * 3 * ff, ff2)], weight.at[rows, lanes]))
    copies = gather_pieces(pieces, sems)
    squares = jnp.sum(second[:, cols : cols + 8].astype(f32), axis=0).T
    squares = squares[:, 0:1] + squares[:, 1:2]
    high = squares.astype(bf16).astype(f32)
    lane = lax.broadcasted_iota(jnp.int32, (squares.shape[0], 128), 1)
    total[:, 2 * span :] = jnp.where(
        lane == 0, high, jnp.where(lane == 1, squares - high, 0.0)
    )
    wait_all(copies[:Z])
    for s in range(Y):
        y = at_y if s == 0 else 1 - at_y
        for d in range(X):
            i = s * X + d
            if i % both == 0:
                wait_all(copies[Z + 2 * i : Z + 2 * (i + both)])
            got = jnp.dot(
                weight[i * ff2 : (i + 1) * ff2], normed[...], preferred_element_type=f32
            )
            block = (y * X + (at_x + X - d) % X) * ff
            columns[pl.ds(offset(block, 16), ff)] = got[:ff]
            columns[pl.ds(offset(span + block, 16), ff)] = got[ff:]
    step = 384
    for i in range(2 * span // step):
        rows = slice(i * step, (i + 1) * step)
        total[:, rows] = columns[rows].T
    for e, out in enumerate((own_out, o1, o2, o3)):
        to = (at_x + e) % X
        for z in range(0, Z, 2):
            pair = [total[pl.ds(offset(((z + i) * X + to) * 8, 8), 8)] for i in range(2)]
            out[z * 8 : (z + 2) * 8] = jnp.concatenate(pair, axis=0).astype(out.dtype)


def act_kernel(width, own, r1, r2, r3, hidden):
    span = hidden.shape[1]
    summed = own[...] + r1[...].astype(f32) + r2[...].astype(f32) + r3[...].astype(f32)
    squares = summed[:, 2 * span : 2 * span + 1] + summed[:, 2 * span + 1 : 2 * span + 2]
    scale = lax.rsqrt(squares / width + norm_eps)
    gate, up = summed[:, :span] * scale, summed[:, span : 2 * span] * scale
    hidden[...] = (gate / (1.0 + jnp.exp(-gate)) * up).astype(bf16)


def down_kernel(
    at, h0, h1, h2, h3, proj, w0, w1, w2, w3, f0, f1, f2, f3, out, weight, act, total, sems
):
    at_x, at_z, at_y = at[1], at[2], at[3]
    both, half = X // 2, w0.shape[1]
    width = 2 * half
    ff = w0.shape[0] // (3 * both)
    rows = h0.shape[0]
    pieces = []
    for i, (which, c) in enumerate(sources_of(at, (w0, w1, w2, w3), (f0, f1, f2, f3))):
        lanes = pl.ds(offset(c * half, 128), half)
        y = at_y if i // 4 == 0 else 1 - at_y
        for j in range(both):
            d = i // 2 % 2 * both + j
            block = (y * X + (at_x + X - d) % X) * ff
            pieces.append(
                (
                    which.at[pl.ds((3 * j + 2) * ff, ff)],
                    weight.at[pl.ds(offset(block, 16), ff), lanes],
                )
            )
    copies = gather_pieces(pieces, sems)
    for e, h in enumerate((h0, h1, h2, h3)):
        act[pl.ds(offset((at_x + X - e) % X * rows, 16), rows)] = h[...]
    spot = at_z * 224
    base = jnp.minimum(spot // 128 * 128, width - 384)
    row = lax.broadcasted_iota(jnp.int32, (256, 384), 0)
    lane = lax.broadcasted_iota(jnp.int32, (256, 384), 1)
    pick = jnp.where(row < 224, (row + (spot - base) == lane).astype(f32), 0.0).astype(bf16)
    placed = jnp.dot(proj[...].astype(bf16), pick, preferred_element_type=f32)
    wait_all(copies)
    total[...] = jnp.dot(act[...], weight[...], preferred_element_type=f32)
    lanes = pl.ds(offset(base, 128), 384)
    for x in range(X):
        mine = [placed[(z * X + x) * 8 : (z * X + x + 1) * 8] for z in range(Z)]
        total[x * rows : (x + 1) * rows, lanes] += jnp.concatenate(mine, axis=0)
    out[...] = total[...].astype(bf16)


def shifted(value, axis, step):
    size = lax.axis_size(axis)
    return lax.ppermute(value, axis, [(i, (i + step) % size) for i in range(size)])


def around(low, high):
    size = lax.axis_size("role") * Y
    up = [(i, (i + 1) % size) for i in range(size)]
    return (
        lax.ppermute(low, ("role", "y"), up),
        lax.ppermute(high, ("role", "y"), [(b, a) for a, b in up]),
    )


def pair(values):
    return [shifted(value, "pair", 1) for value in values]


def after(values, *others):
    return lax.optimization_barrier((values, others))[0]


def lanes(weight, begin, size):
    return lax.dynamic_slice_in_dim(weight, begin, size, 1)


def per_device(
    hidden_in,
    queries,
    new_kv,
    kv_cache,
    block_counts,
    tail_lens,
    block_order,
    out_weight,
    norm_gain,
    gate_weight,
    up_weight,
    down_weight,
):
    core, at_x, at_z, at_y = (lax.axis_index(a) for a in ("pair", "x", "z", "y"))
    at = jnp.stack([core, at_x, at_z, at_y])
    rows, width = hidden_in.shape
    slab = width // X
    block = width // (X * Z * Y)
    cols = Y * block
    chunk = X * Z * rows
    ff = gate_weight.shape[1]
    span = X * Y * ff
    heads = queries.shape[1] // X
    out_t, gate_t, up_t = out_weight.T, gate_weight.T, up_weight.T

    half = heads // 2
    pieces = [lanes(out_t, (at_x + d) % X * heads + core * half, half) for d in range(X)]
    out_pieces = [pieces[0]] + [shifted(pieces[d], "x", d) for d in range(1, X)]
    gain = shifted(norm_gain, "y", 1)
    gain = jnp.where(
        at_y == 0, jnp.concatenate([norm_gain, gain]), jnp.concatenate([gain, norm_gain])
    )[:, None]

    attended = attend(queries, new_kv, kv_cache, block_counts, tail_lens, block_order)
    first = jnp.concatenate(
        [attended.reshape(rows, X, heads), hidden_in.reshape(rows, X, slab)], axis=2
    ).transpose(1, 0, 2)
    first = after(first, (out_pieces, gain))
    pieces = cut(at, *after((gate_t, up_t, down_weight), first))
    first = lax.all_to_all(first, "x", 0, 0, tiled=True).reshape(X * rows, heads + slab)
    resid = first[:, heads:].reshape(X * rows, Z, cols).transpose(1, 0, 2)
    resid = jnp.pad(resid, ((0, 0), (0, 0), (0, 256 - cols)))
    first = jnp.concatenate(
        [jnp.broadcast_to(first[None, :, :heads], (Z, X * rows, heads)), resid], axis=2
    )
    first = lax.all_to_all(first, "z", 0, 0, tiled=True).reshape(chunk, heads + 256)

    out_near = join(out_pieces)
    out_side = shifted(out_near, "y", 1)
    out_all = [out_near, *pair([out_near]), out_side, *pair([out_side])]
    moved = [shifted(pieces[1], "x", 1), shifted(pieces[3], "x", -1)]
    across = shifted(after(pieces[2], moved), "x", 2)

    own, *sends = call(
        project_kernel,
        [jax.ShapeDtypeStruct((cols, chunk), t) for t in (f32, bf16, bf16, bf16)],
        [smem()] + [anywhere()] * 5,
        [
            pltpu.VMEM((X * cols, heads), bf16),
            pltpu.VMEM((chunk, heads), bf16),
            pltpu.SemaphoreType.DMA((5,)),
        ],
        (2 * X * cols * chunk * heads, X * cols * heads * 4),
        58,
    )(at, first, *out_all)
    received = [shifted(send, "x", -d) for d, send in enumerate(sends, 1)]
    weights = [join([pieces[0], moved[0]]), join([after(across, own), moved[1]])]
    weights += around(*weights)
    second, proj = call(
        norm_kernel,
        [
            jax.ShapeDtypeStruct((Z, cols + 8, chunk), bf16),
            jax.ShapeDtypeStruct((chunk, 256), f32),
        ],
        [vmem()] * 6,
        [],
        (10 * cols * chunk, 20 * cols * chunk),
        58,
    )(first, own, *received, gain)
    weights = after(weights, second)
    weights += pair(weights)
    second = lax.all_to_all(second, "z", 0, 0, tiled=True)

    message = (Z * rows, 2 * span + 128)
    own, *sends = call(
        gate_up_kernel,
        [jax.ShapeDtypeStruct(message, t) for t in (f32, bf16, bf16, bf16)],
        [smem(), vmem()] + [anywhere()] * 8,
        [
            pltpu.VMEM((2 * span, slab), bf16),
            pltpu.VMEM((slab, chunk), bf16),
            pltpu.VMEM((2 * span, chunk), f32),
            pltpu.VMEM((chunk, message[1]), f32),
            pltpu.SemaphoreType.DMA((16 + Z,)),
        ],
        (4 * span * slab * chunk, 2 * span * slab * 4),
        58,
    )(at, second, *weights)
    received = [shifted(send, "x", e) for e, send in enumerate(sends, 1)]
    hidden = call(
        lambda *refs: act_kernel(width, *refs),
        jax.ShapeDtypeStruct((Z * rows, span), bf16),
        [vmem()] * 4,
        [],
        (20 * span * Z * rows, 20 * span * Z * rows),
        8,
    )(own, *received)
    hidden = [hidden] + [shifted(hidden, "x", e) for e in range(1, X)]
    result = call(
        down_kernel,
        jax.ShapeDtypeStruct((chunk, slab), bf16),
        [smem()] + [vmem()] * 5 + [anywhere()] * 8,
        [
            pltpu.VMEM((span, slab), bf16),
            pltpu.VMEM((chunk, span), bf16),
            pltpu.VMEM((chunk, slab), f32),
            pltpu.SemaphoreType.DMA((16,)),
        ],
        (2 * span * chunk * slab, span * slab * 4),
        58,
    )(at, *hidden, proj, *weights)
    result = result.reshape(X * Z, rows, slab)
    result = lax.all_to_all(result, ("x", "z"), 0, 0, tiled=True).reshape(X, Z, rows, slab)
    result = jnp.sum(result.astype(f32), axis=1)
    result = result.transpose(1, 0, 2).reshape(rows, width)
    return (result + hidden_in.astype(f32)).astype(bf16)


def solution(mesh):
    fine = Mesh(mesh.devices.reshape(2, 2, X, Z, Y), ("role", "pair", "x", "z", "y"))
    dev = ("x", "z", "y")
    every = ("role", "pair") + dev
    return jax.shard_map(
        per_device,
        mesh=fine,
        in_specs=(
            P(every, None),
            P(every, None),
            P(every, None),
            P(every, None, None),
            P(every, None),
            P(every),
            P(every, None),
            P(None, dev),
            P(dev),
            P(None, dev),
            P(None, dev),
            P(dev, None),
        ),
        out_specs=P(every, None),
        check_vma=False,
    )
```

```python
import jax
import jax.numpy as jnp
from jax import lax
from jax.experimental import pallas as pl
from jax.experimental.pallas import tpu as pltpu
from jax.sharding import Mesh, PartitionSpec as P

norm_eps = 1e-05
X, Z, Y = 4, 8, 2
LINE = Z * Y
f32, bf16 = jnp.float32, jnp.bfloat16
NT = (((1,), (1,)), ((), ()))
MIB = 1024 * 1024


def smem():
    return pl.BlockSpec(memory_space=pltpu.SMEM)


def vmem():
    return pl.BlockSpec(memory_space=pltpu.VMEM)


def anywhere():
    return pl.BlockSpec(memory_space=pl.ANY)


def call(kernel, outs, ins, scratch, cost, mib):
    single = not isinstance(outs, (list, tuple))
    return pl.pallas_call(
        kernel,
        out_shape=outs,
        in_specs=ins,
        out_specs=vmem() if single else [vmem()] * len(outs),
        scratch_shapes=scratch,
        compiler_params=pltpu.CompilerParams(vmem_limit_bytes=mib * MIB),
        cost_estimate=pl.CostEstimate(flops=cost[0], bytes_accessed=cost[1], transcendentals=0),
    )


def gather_pieces(pieces, sems):
    copies = [
        pltpu.make_async_copy(source, target, sems.at[i]) for i, (source, target) in enumerate(pieces)
    ]
    for copy in copies:
        copy.start()
    return copies


def wait_all(copies):
    for copy in copies:
        copy.wait()


def offset(value, unit):
    return pl.multiple_of(value, unit)


def cut_kernel(at, gate, up, down, p0, p1, p2, p3, sems):
    core, at_x = at[0], at[1]
    ff, half = gate.shape[0], p0.shape[1]
    pieces = []
    for d, out in ((1, p1), (3, p3), (2, p2), (0, p0)):
        begin = offset((at_x + d) % X * (2 * half) + core * half, 128)
        for part, source in enumerate((gate, up, down)):
            pieces.append((source.at[:, pl.ds(begin, half)], out.at[pl.ds(part * ff, ff)]))
    wait_all(gather_pieces(pieces, sems))


def cut(at, gate_t, up_t, down):
    ff, width = gate_t.shape
    return call(
        cut_kernel,
        [jax.ShapeDtypeStruct((3 * ff, width // X // 2), bf16)] * X,
        [smem()] + [anywhere()] * 3,
        [pltpu.SemaphoreType.DMA((3 * X,))],
        (0, 6 * ff * width),
        58,
    )(at, gate_t, up_t, down)


def attend_kernel(
    counts, tails, order, q_ref, new_ref, kv_ref, out_ref, score, top, total, mixed
):
    rows, heads, size = q_ref.shape
    pool, block, _ = kv_ref.shape
    scale = size ** (-0.5)
    owner, limit = [], []
    row, rank = jnp.int32(0), jnp.int32(0)
    for p in range(pool):
        last = rank + 1 == counts[0, row]
        owner.append(row)
        limit.append(jnp.where(last, tails[row], block))
        row = jnp.minimum(jnp.where(last, row + 1, row), rows - 1)
        rank = jnp.where(last, 0, rank + 1)
    own = []
    for r in range(rows):
        key = new_ref[r : r + 1, :size].astype(f32)
        own.append(jnp.sum(q_ref[r].astype(f32) * key, axis=1, keepdims=True) * scale)
        top[r] = jnp.broadcast_to(own[r], (heads, 128))
    lane = lax.broadcasted_iota(jnp.int32, (heads, block), 1)
    for p in range(pool):
        s = lax.dot_general(
            q_ref[owner[p]], kv_ref[order[0, p], :, :size], NT, preferred_element_type=f32
        )
        s = jnp.where(lane < limit[p], s * scale, -jnp.inf)
        score[p] = s
        top[owner[p]] = jnp.maximum(top[owner[p]], jnp.max(s, axis=1, keepdims=True))
    for r in range(rows):
        weight = jnp.exp(own[r] - top[r][:, :1])
        total[r] = jnp.broadcast_to(weight, (heads, 128))
        mixed[r] = weight * new_ref[r : r + 1, size:].astype(f32)
    for p in range(pool):
        weight = jnp.exp(score[p] - top[owner[p]][:, :1])
        total[owner[p]] += jnp.sum(weight, axis=1, keepdims=True)
        mixed[owner[p]] += jnp.dot(
            weight.astype(bf16), kv_ref[order[0, p], :, size:], preferred_element_type=f32
        )
    for r in range(rows):
        out_ref[r] = (mixed[r] / total[r][:, :1]).astype(bf16)


def attend(queries, new_kv, kv_cache, block_counts, tail_lens, block_order):
    rows = queries.shape[0]
    pool, block, twice = kv_cache.shape
    size = twice // 2
    heads = queries.shape[1] // size
    mixed = call(
        attend_kernel,
        jax.ShapeDtypeStruct((rows, heads, size), bf16),
        [smem()] * 3 + [vmem()] * 3,
        [
            pltpu.VMEM((pool, heads, block), f32),
            pltpu.VMEM((rows, heads, 128), f32),
            pltpu.VMEM((rows, heads, 128), f32),
            pltpu.VMEM((rows, heads, size), f32),
        ],
        (4 * pool * heads * block * size, pool * block * twice * 2),
        58,
    )(block_counts, tail_lens, block_order, queries.reshape(rows, heads, size), new_kv, kv_cache)
    return mixed.reshape(rows, heads * size)


def join_kernel(*refs):
    sources, out, sems = refs[:-2], refs[-2], refs[-1]
    pieces, row = [], 0
    for source in sources:
        pieces.append((source, out.at[pl.ds(row, source.shape[0])]))
        row += source.shape[0]
    wait_all(gather_pieces(pieces, sems))


def join(pieces):
    shape = (sum(piece.shape[0] for piece in pieces), pieces[0].shape[1])
    return call(
        join_kernel,
        jax.ShapeDtypeStruct(shape, bf16),
        [anywhere()] * len(pieces),
        [pltpu.SemaphoreType.DMA((len(pieces),))],
        (0, shape[0] * shape[1] * 4),
        58,
    )(*pieces)


def project_kernel(
    at, first, near, near_far, side, side_far, own_out, o1, o2, o3, weight, heads, sems
):
    core, at_y = at[0], at[3]
    cols, half = near.shape[0] // X, near.shape[1]
    width = 2 * half
    pieces = [(first.at[:, pl.ds(0, width)], heads)]
    for which, c, y in (
        (near, core, at_y),
        (side, core, 1 - at_y),
        (near_far, 1 - core, at_y),
        (side_far, 1 - core, 1 - at_y),
    ):
        rows = pl.ds(offset(y * X * cols, 16), X * cols)
        pieces.append((which, weight.at[rows, pl.ds(offset(c * half, 128), half)]))
    wait_all(gather_pieces(pieces, sems))
    for y in range(Y):
        got = lax.dot_general(
            weight[y * X * cols : (y + 1) * X * cols], heads[...], NT, preferred_element_type=f32
        )
        for d, out in enumerate((own_out, o1, o2, o3)):
            out[y * cols : (y + 1) * cols] = got[d * cols : (d + 1) * cols].astype(out.dtype)


def norm_kernel(first, own, r1, r2, r3, gain, second, proj_out):
    cols = own.shape[0]
    width = first.shape[1] - 256
    proj = own[...] + r1[...].astype(f32) + r2[...].astype(f32) + r3[...].astype(f32)
    resid = first[:, width:].astype(f32).T
    stream = proj + resid[:cols]
    squares = jnp.sum(stream * stream, axis=0, keepdims=True)
    high = squares.astype(bf16).astype(f32)
    line = lax.broadcasted_iota(jnp.int32, (16, stream.shape[1]), 0)
    tail = jnp.where(line == 0, high, jnp.where(line == 1, squares - high, 0.0)).astype(bf16)
    scaled = (stream * gain[...]).astype(bf16)
    for z in range(Z):
        second[z, :cols] = scaled
        second[z, cols:] = tail
    proj_out[...] = jnp.concatenate(
        [proj, jnp.zeros((256 - cols, proj.shape[1]), f32)], axis=0
    ).T


def sources_of(at, own, far):
    return [(which, c) for a, b in zip(own, far) for which, c in ((a, at[0]), (b, 1 - at[0]))]


def gate_up_kernel(
    at, second, w0, w1, w2, w3, f0, f1, f2, f3,
    own_out, o1, o2, o3, weight, normed, columns, total, sems,
):
    at_x, at_y = at[1], at[3]
    both, half = X // 2, w0.shape[1]
    ff = w0.shape[0] // (3 * both)
    ff2 = 2 * ff
    span = X * Y * ff
    cols = normed.shape[0] // Z
    pieces = [
        (second.at[z, pl.ds(0, cols)], normed.at[pl.ds(z * cols, cols)]) for z in range(Z)
    ]
    for i, (which, c) in enumerate(sources_of(at, (w0, w1, w2, w3), (f0, f1, f2, f3))):
        lanes = pl.ds(offset(c * half, 128), half)
        for j in range(both):
            rows = pl.ds((i // 2 * both + j) * ff2, ff2)
            pieces.append((which.at[pl.ds(j * 3 * ff, ff2)], weight.at[rows, lanes]))
    copies = gather_pieces(pieces, sems)
    squares = jnp.sum(second[:, cols : cols + 16].astype(f32), axis=0).T
    squares = squares[:, 0:1] + squares[:, 1:2]
    high = squares.astype(bf16).astype(f32)
    lane = lax.broadcasted_iota(jnp.int32, (squares.shape[0], 128), 1)
    total[:, 2 * span :] = jnp.where(
        lane == 0, high, jnp.where(lane == 1, squares - high, 0.0)
    )
    wait_all(copies[:Z])
    for s in range(Y):
        y = at_y if s == 0 else 1 - at_y
        for d in range(X):
            i = s * X + d
            if i % both == 0:
                wait_all(copies[Z + 2 * i : Z + 2 * (i + both)])
            got = jnp.dot(
                weight[i * ff2 : (i + 1) * ff2], normed[...], preferred_element_type=f32
            )
            block = (y * X + (at_x + X - d) % X) * ff
            columns[pl.ds(offset(block, 16), ff)] = got[:ff]
            columns[pl.ds(offset(span + block, 16), ff)] = got[ff:]
    step = 384
    for i in range(2 * span // step):
        rows = slice(i * step, (i + 1) * step)
        total[:, rows] = columns[rows].T
    for e, out in enumerate((own_out, o1, o2, o3)):
        to = (at_x + e) % X
        for z in range(0, Z, 2):
            pair = [total[pl.ds(offset(((z + i) * X + to) * 8, 8), 8)] for i in range(2)]
            out[z * 8 : (z + 2) * 8] = jnp.concatenate(pair, axis=0).astype(out.dtype)


def act_kernel(width, own, r1, r2, r3, hidden):
    span = hidden.shape[1]
    summed = own[...] + r1[...].astype(f32) + r2[...].astype(f32) + r3[...].astype(f32)
    squares = summed[:, 2 * span : 2 * span + 1] + summed[:, 2 * span + 1 : 2 * span + 2]
    scale = lax.rsqrt(squares / width + norm_eps)
    gate, up = summed[:, :span] * scale, summed[:, span : 2 * span] * scale
    hidden[...] = (gate / (1.0 + jnp.exp(-gate)) * up).astype(bf16)


def down_kernel(
    at, h0, h1, h2, h3, proj, w0, w1, w2, w3, f0, f1, f2, f3, out, weight, act, total, sems
):
    at_x, at_z, at_y = at[1], at[2], at[3]
    both, half = X // 2, w0.shape[1]
    width = 2 * half
    ff = w0.shape[0] // (3 * both)
    rows = h0.shape[0]
    pieces = []
    for i, (which, c) in enumerate(sources_of(at, (w0, w1, w2, w3), (f0, f1, f2, f3))):
        lanes = pl.ds(offset(c * half, 128), half)
        y = at_y if i // 4 == 0 else 1 - at_y
        for j in range(both):
            d = i // 2 % 2 * both + j
            block = (y * X + (at_x + X - d) % X) * ff
            pieces.append(
                (
                    which.at[pl.ds((3 * j + 2) * ff, ff)],
                    weight.at[pl.ds(offset(block, 16), ff), lanes],
                )
            )
    copies = gather_pieces(pieces, sems)
    for e, h in enumerate((h0, h1, h2, h3)):
        act[pl.ds(offset((at_x + X - e) % X * rows, 16), rows)] = h[...]
    spot = at_z * 224
    base = jnp.minimum(spot // 128 * 128, width - 384)
    row = lax.broadcasted_iota(jnp.int32, (256, 384), 0)
    lane = lax.broadcasted_iota(jnp.int32, (256, 384), 1)
    pick = jnp.where(row < 224, (row + (spot - base) == lane).astype(f32), 0.0).astype(bf16)
    placed = jnp.dot(proj[...].astype(bf16), pick, preferred_element_type=f32)
    wait_all(copies)
    total[...] = jnp.dot(act[...], weight[...], preferred_element_type=f32)
    lanes = pl.ds(offset(base, 128), 384)
    for x in range(X):
        mine = [placed[(z * X + x) * 8 : (z * X + x + 1) * 8] for z in range(Z)]
        total[x * rows : (x + 1) * rows, lanes] += jnp.concatenate(mine, axis=0)
    out[...] = total[...].astype(bf16)


def shifted(value, axis, step):
    size = lax.axis_size(axis)
    return lax.ppermute(value, axis, [(i, (i + step) % size) for i in range(size)])


def around(low, high):
    size = lax.axis_size("role") * Y
    up = [(i, (i + 1) % size) for i in range(size)]
    return (
        lax.ppermute(low, ("role", "y"), up),
        lax.ppermute(high, ("role", "y"), [(b, a) for a, b in up]),
    )


def pair(values):
    return [shifted(value, "pair", 1) for value in values]


def after(values, *others):
    return lax.optimization_barrier((values, others))[0]


def lanes(weight, begin, size):
    return lax.dynamic_slice_in_dim(weight, begin, size, 1)


def per_device(
    hidden_in,
    queries,
    new_kv,
    kv_cache,
    block_counts,
    tail_lens,
    block_order,
    out_weight,
    norm_gain,
    gate_weight,
    up_weight,
    down_weight,
):
    core, at_x, at_z, at_y = (lax.axis_index(a) for a in ("pair", "x", "z", "y"))
    at = jnp.stack([core, at_x, at_z, at_y])
    rows, width = hidden_in.shape
    slab = width // X
    block = width // (X * Z * Y)
    cols = Y * block
    chunk = X * Z * rows
    ff = gate_weight.shape[1]
    span = X * Y * ff
    heads = queries.shape[1] // X
    out_t, gate_t, up_t = out_weight.T, gate_weight.T, up_weight.T

    half = heads // 2
    pieces = [lanes(out_t, (at_x + d) % X * heads + core * half, half) for d in range(X)]
    out_pieces = [pieces[0]] + [shifted(pieces[d], "x", d) for d in range(1, X)]
    gain = shifted(norm_gain, "y", 1)
    gain = jnp.where(
        at_y == 0, jnp.concatenate([norm_gain, gain]), jnp.concatenate([gain, norm_gain])
    )[:, None]

    attended = attend(queries, new_kv, kv_cache, block_counts, tail_lens, block_order)
    first = jnp.concatenate(
        [attended.reshape(rows, X, heads), hidden_in.reshape(rows, X, slab)], axis=2
    ).transpose(1, 0, 2)
    first = after(first, (out_pieces, gain))
    pieces = cut(at, *after((gate_t, up_t, down_weight), first))
    first = lax.all_to_all(first, "x", 0, 0, tiled=True).reshape(X * rows, heads + slab)
    resid = first[:, heads:].reshape(X * rows, Z, cols).transpose(1, 0, 2)
    resid = jnp.pad(resid, ((0, 0), (0, 0), (0, 256 - cols)))
    first = jnp.concatenate(
        [jnp.broadcast_to(first[None, :, :heads], (Z, X * rows, heads)), resid], axis=2
    )
    first = lax.all_to_all(first, "z", 0, 0, tiled=True).reshape(chunk, heads + 256)

    out_near = join(out_pieces)
    out_side = shifted(out_near, "y", 1)
    out_all = [out_near, *pair([out_near]), out_side, *pair([out_side])]
    moved = [shifted(pieces[1], "x", 1), shifted(pieces[3], "x", -1)]
    across = shifted(after(pieces[2], moved), "x", 2)

    own, *sends = call(
        project_kernel,
        [jax.ShapeDtypeStruct((cols, chunk), t) for t in (f32, bf16, bf16, bf16)],
        [smem()] + [anywhere()] * 5,
        [
            pltpu.VMEM((X * cols, heads), bf16),
            pltpu.VMEM((chunk, heads), bf16),
            pltpu.SemaphoreType.DMA((5,)),
        ],
        (2 * X * cols * chunk * heads, X * cols * heads * 4),
        58,
    )(at, first, *out_all)
    received = [shifted(send, "x", -d) for d, send in enumerate(sends, 1)]
    weights = [join([pieces[0], moved[0]]), join([after(across, own), moved[1]])]
    weights += around(*weights)
    second, proj = call(
        norm_kernel,
        [
            jax.ShapeDtypeStruct((Z, cols + 16, chunk), bf16),
            jax.ShapeDtypeStruct((chunk, 256), f32),
        ],
        [vmem()] * 6,
        [],
        (10 * cols * chunk, 20 * cols * chunk),
        8,
    )(first, own, *received, gain)
    weights = after(weights, second)
    weights += pair(weights)
    second = lax.all_to_all(second, "z", 0, 0, tiled=True)

    message = (Z * rows, 2 * span + 128)
    own, *sends = call(
        gate_up_kernel,
        [jax.ShapeDtypeStruct(message, t) for t in (f32, bf16, bf16, bf16)],
        [smem(), vmem()] + [anywhere()] * 8,
        [
            pltpu.VMEM((2 * span, slab), bf16),
            pltpu.VMEM((slab, chunk), bf16),
            pltpu.VMEM((2 * span, chunk), f32),
            pltpu.VMEM((chunk, message[1]), f32),
            pltpu.SemaphoreType.DMA((16 + Z,)),
        ],
        (4 * span * slab * chunk, 2 * span * slab * 4),
        26,
    )(at, second, *weights)
    received = [shifted(send, "x", e) for e, send in enumerate(sends, 1)]
    hidden = call(
        lambda *refs: act_kernel(width, *refs),
        jax.ShapeDtypeStruct((Z * rows, span), bf16),
        [vmem()] * 4,
        [],
        (20 * span * Z * rows, 20 * span * Z * rows),
        8,
    )(own, *received)
    hidden = [hidden] + [shifted(hidden, "x", e) for e in range(1, X)]
    result = call(
        down_kernel,
        jax.ShapeDtypeStruct((chunk, slab), bf16),
        [smem()] + [vmem()] * 5 + [anywhere()] * 8,
        [
            pltpu.VMEM((span, slab), bf16),
            pltpu.VMEM((chunk, span), bf16),
            pltpu.VMEM((chunk, slab), f32),
            pltpu.SemaphoreType.DMA((16,)),
        ],
        (2 * span * chunk * slab, span * slab * 4),
        20,
    )(at, *hidden, proj, *weights)
    result = result.reshape(X * Z, rows, slab)
    result = lax.all_to_all(result, ("x", "z"), 0, 0, tiled=True).reshape(X, Z, rows, slab)
    result = jnp.sum(result.astype(f32), axis=1)
    result = result.transpose(1, 0, 2).reshape(rows, width)
    return (result + hidden_in.astype(f32)).astype(bf16)


def solution(mesh):
    fine = Mesh(mesh.devices.reshape(2, 2, X, Z, Y), ("role", "pair", "x", "z", "y"))
    dev = ("x", "z", "y")
    every = ("role", "pair") + dev
    return jax.shard_map(
        per_device,
        mesh=fine,
        in_specs=(
            P(every, None),
            P(every, None),
            P(every, None),
            P(every, None, None),
            P(every, None),
            P(every),
            P(every, None),
            P(None, dev),
            P(dev),
            P(None, dev),
            P(None, dev),
            P(dev, None),
        ),
        out_specs=P(every, None),
        check_vma=False,
    )
```

```python
import jax
import jax.numpy as jnp
from jax import lax
from jax.experimental import pallas as pl
from jax.experimental.pallas import tpu as pltpu
from jax.sharding import Mesh, PartitionSpec as P

norm_eps = 1e-05
X, Z, Y = 4, 8, 2
LINE = Z * Y
f32, bf16 = jnp.float32, jnp.bfloat16
NT = (((1,), (1,)), ((), ()))
MIB = 1024 * 1024


def smem():
    return pl.BlockSpec(memory_space=pltpu.SMEM)


def vmem():
    return pl.BlockSpec(memory_space=pltpu.VMEM)


def anywhere():
    return pl.BlockSpec(memory_space=pl.ANY)


def call(kernel, outs, ins, scratch, cost, mib):
    single = not isinstance(outs, (list, tuple))
    return pl.pallas_call(
        kernel,
        out_shape=outs,
        in_specs=ins,
        out_specs=vmem() if single else [vmem()] * len(outs),
        scratch_shapes=scratch,
        compiler_params=pltpu.CompilerParams(vmem_limit_bytes=mib * MIB),
        cost_estimate=pl.CostEstimate(flops=cost[0], bytes_accessed=cost[1], transcendentals=0),
    )


def gather_pieces(pieces, sems):
    copies = [
        pltpu.make_async_copy(source, target, sems.at[i]) for i, (source, target) in enumerate(pieces)
    ]
    for copy in copies:
        copy.start()
    return copies


def wait_all(copies):
    for copy in copies:
        copy.wait()


def offset(value, unit):
    return pl.multiple_of(value, unit)


def cut_kernel(at, gate, up, down, p0, p1, p2, p3, sems):
    core, at_x = at[0], at[1]
    ff, half = gate.shape[0], p0.shape[1]
    pieces = []
    for d, out in ((1, p1), (3, p3), (2, p2), (0, p0)):
        begin = offset((at_x + d) % X * (2 * half) + core * half, 128)
        for part, source in enumerate((gate, up, down)):
            pieces.append((source.at[:, pl.ds(begin, half)], out.at[pl.ds(part * ff, ff)]))
    wait_all(gather_pieces(pieces, sems))


def cut(at, gate_t, up_t, down):
    ff, width = gate_t.shape
    return call(
        cut_kernel,
        [jax.ShapeDtypeStruct((3 * ff, width // X // 2), bf16)] * X,
        [smem()] + [anywhere()] * 3,
        [pltpu.SemaphoreType.DMA((3 * X,))],
        (0, 6 * ff * width),
        58,
    )(at, gate_t, up_t, down)


def attend_kernel(
    counts, tails, order, q_ref, new_ref, kv_ref, out_ref, score, top, total, mixed
):
    rows, heads, size = q_ref.shape
    pool, block, _ = kv_ref.shape
    scale = size ** (-0.5)
    owner, limit = [], []
    row, rank = jnp.int32(0), jnp.int32(0)
    for p in range(pool):
        last = rank + 1 == counts[0, row]
        owner.append(row)
        limit.append(jnp.where(last, tails[row], block))
        row = jnp.minimum(jnp.where(last, row + 1, row), rows - 1)
        rank = jnp.where(last, 0, rank + 1)
    own = []
    for r in range(rows):
        key = new_ref[r : r + 1, :size].astype(f32)
        own.append(jnp.sum(q_ref[r].astype(f32) * key, axis=1, keepdims=True) * scale)
        top[r] = jnp.broadcast_to(own[r], (heads, 128))
    lane = lax.broadcasted_iota(jnp.int32, (heads, block), 1)
    for p in range(pool):
        s = lax.dot_general(
            q_ref[owner[p]], kv_ref[order[0, p], :, :size], NT, preferred_element_type=f32
        )
        s = jnp.where(lane < limit[p], s * scale, -jnp.inf)
        score[p] = s
        top[owner[p]] = jnp.maximum(top[owner[p]], jnp.max(s, axis=1, keepdims=True))
    for r in range(rows):
        weight = jnp.exp(own[r] - top[r][:, :1])
        total[r] = jnp.broadcast_to(weight, (heads, 128))
        mixed[r] = weight * new_ref[r : r + 1, size:].astype(f32)
    for p in range(pool):
        weight = jnp.exp(score[p] - top[owner[p]][:, :1])
        total[owner[p]] += jnp.sum(weight, axis=1, keepdims=True)
        mixed[owner[p]] += jnp.dot(
            weight.astype(bf16), kv_ref[order[0, p], :, size:], preferred_element_type=f32
        )
    for r in range(rows):
        out_ref[r] = (mixed[r] / total[r][:, :1]).astype(bf16)


def attend(queries, new_kv, kv_cache, block_counts, tail_lens, block_order):
    rows = queries.shape[0]
    pool, block, twice = kv_cache.shape
    size = twice // 2
    heads = queries.shape[1] // size
    mixed = call(
        attend_kernel,
        jax.ShapeDtypeStruct((rows, heads, size), bf16),
        [smem()] * 3 + [vmem()] * 3,
        [
            pltpu.VMEM((pool, heads, block), f32),
            pltpu.VMEM((rows, heads, 128), f32),
            pltpu.VMEM((rows, heads, 128), f32),
            pltpu.VMEM((rows, heads, size), f32),
        ],
        (4 * pool * heads * block * size, pool * block * twice * 2),
        58,
    )(block_counts, tail_lens, block_order, queries.reshape(rows, heads, size), new_kv, kv_cache)
    return mixed.reshape(rows, heads * size)


def join_kernel(*refs):
    sources, out, sems = refs[:-2], refs[-2], refs[-1]
    pieces, row = [], 0
    for source in sources:
        pieces.append((source, out.at[pl.ds(row, source.shape[0])]))
        row += source.shape[0]
    wait_all(gather_pieces(pieces, sems))


def join(pieces):
    shape = (sum(piece.shape[0] for piece in pieces), pieces[0].shape[1])
    return call(
        join_kernel,
        jax.ShapeDtypeStruct(shape, bf16),
        [anywhere()] * len(pieces),
        [pltpu.SemaphoreType.DMA((len(pieces),))],
        (0, shape[0] * shape[1] * 4),
        58,
    )(*pieces)


def project_kernel(
    at, first, near, near_far, side, side_far, own_out, o1, o2, o3, weight, heads, sems
):
    core, at_y = at[0], at[3]
    cols, half = near.shape[0] // X, near.shape[1]
    width = 2 * half
    pieces = [(first.at[:, pl.ds(0, width)], heads)]
    for which, c, y in (
        (near, core, at_y),
        (side, core, 1 - at_y),
        (near_far, 1 - core, at_y),
        (side_far, 1 - core, 1 - at_y),
    ):
        rows = pl.ds(offset(y * X * cols, 16), X * cols)
        pieces.append((which, weight.at[rows, pl.ds(offset(c * half, 128), half)]))
    wait_all(gather_pieces(pieces, sems))
    for y in range(Y):
        got = lax.dot_general(
            weight[y * X * cols : (y + 1) * X * cols], heads[...], NT, preferred_element_type=f32
        )
        for d, out in enumerate((own_out, o1, o2, o3)):
            out[y * cols : (y + 1) * cols] = got[d * cols : (d + 1) * cols].astype(out.dtype)


def norm_kernel(first, own, r1, r2, r3, gain, second, proj_out):
    cols = own.shape[0]
    width = first.shape[1] - 256
    proj = own[...] + r1[...].astype(f32) + r2[...].astype(f32) + r3[...].astype(f32)
    resid = first[:, width:].astype(f32).T
    stream = proj + resid[:cols]
    squares = jnp.sum(stream * stream, axis=0, keepdims=True)
    high = squares.astype(bf16).astype(f32)
    line = lax.broadcasted_iota(jnp.int32, (16, stream.shape[1]), 0)
    tail = jnp.where(line == 0, high, jnp.where(line == 1, squares - high, 0.0)).astype(bf16)
    scaled = (stream * gain[...]).astype(bf16)
    for z in range(Z):
        second[z, :cols] = scaled
        second[z, cols:] = tail
    proj_out[...] = jnp.concatenate(
        [proj, jnp.zeros((256 - cols, proj.shape[1]), f32)], axis=0
    ).T


def sources_of(at, own, far):
    return [(which, c) for a, b in zip(own, far) for which, c in ((a, at[0]), (b, 1 - at[0]))]


def gate_up_kernel(
    at, second, w0, w1, w2, w3, f0, f1, f2, f3,
    own_out, o1, o2, o3, weight, normed, columns, total, sems,
):
    at_x, at_y = at[1], at[3]
    both, half = X // 2, w0.shape[1]
    ff = w0.shape[0] // (3 * both)
    ff2 = 2 * ff
    span = X * Y * ff
    cols = normed.shape[0] // Z
    pieces = [
        (second.at[z, pl.ds(0, cols)], normed.at[pl.ds(z * cols, cols)]) for z in range(Z)
    ]
    for i, (which, c) in enumerate(sources_of(at, (w0, w1, w2, w3), (f0, f1, f2, f3))):
        lanes = pl.ds(offset(c * half, 128), half)
        for j in range(both):
            rows = pl.ds((i // 2 * both + j) * ff2, ff2)
            pieces.append((which.at[pl.ds(j * 3 * ff, ff2)], weight.at[rows, lanes]))
    copies = gather_pieces(pieces, sems)
    squares = jnp.sum(second[:, cols : cols + 16].astype(f32), axis=0).T
    squares = squares[:, 0:1] + squares[:, 1:2]
    high = squares.astype(bf16).astype(f32)
    lane = lax.broadcasted_iota(jnp.int32, (squares.shape[0], 128), 1)
    total[:, 2 * span :] = jnp.where(
        lane == 0, high, jnp.where(lane == 1, squares - high, 0.0)
    )
    wait_all(copies[:Z])
    for s in range(Y):
        y = at_y if s == 0 else 1 - at_y
        for d in range(X):
            i = s * X + d
            if i % both == 0:
                wait_all(copies[Z + 2 * i : Z + 2 * (i + both)])
            got = jnp.dot(
                weight[i * ff2 : (i + 1) * ff2], normed[...], preferred_element_type=f32
            )
            block = (y * X + (at_x + X - d) % X) * ff
            columns[pl.ds(offset(block, 16), ff)] = got[:ff]
            columns[pl.ds(offset(span + block, 16), ff)] = got[ff:]
    step = 384
    for i in range(2 * span // step):
        rows = slice(i * step, (i + 1) * step)
        total[:, rows] = columns[rows].T
    for e, out in enumerate((own_out, o1, o2, o3)):
        to = (at_x + e) % X
        for z in range(0, Z, 2):
            pair = [total[pl.ds(offset(((z + i) * X + to) * 8, 8), 8)] for i in range(2)]
            out[z * 8 : (z + 2) * 8] = jnp.concatenate(pair, axis=0).astype(out.dtype)


def act_kernel(width, own, r1, r2, r3, hidden):
    span = hidden.shape[1]
    summed = own[...] + r1[...].astype(f32) + r2[...].astype(f32) + r3[...].astype(f32)
    squares = summed[:, 2 * span : 2 * span + 1] + summed[:, 2 * span + 1 : 2 * span + 2]
    scale = lax.rsqrt(squares / width + norm_eps)
    gate, up = summed[:, :span] * scale, summed[:, span : 2 * span] * scale
    hidden[...] = (gate / (1.0 + jnp.exp(-gate)) * up).astype(bf16)


def down_kernel(
    at, h0, h1, h2, h3, proj, w0, w1, w2, w3, f0, f1, f2, f3, out, weight, act, total, sems
):
    at_x, at_z, at_y = at[1], at[2], at[3]
    both, half = X // 2, w0.shape[1]
    width = 2 * half
    ff = w0.shape[0] // (3 * both)
    rows = h0.shape[0]
    pieces = []
    for i, (which, c) in enumerate(sources_of(at, (w0, w1, w2, w3), (f0, f1, f2, f3))):
        lanes = pl.ds(offset(c * half, 128), half)
        y = at_y if i // 4 == 0 else 1 - at_y
        for j in range(both):
            d = i // 2 % 2 * both + j
            block = (y * X + (at_x + X - d) % X) * ff
            pieces.append(
                (
                    which.at[pl.ds((3 * j + 2) * ff, ff)],
                    weight.at[pl.ds(offset(block, 16), ff), lanes],
                )
            )
    copies = gather_pieces(pieces, sems)
    for e, h in enumerate((h0, h1, h2, h3)):
        act[pl.ds(offset((at_x + X - e) % X * rows, 16), rows)] = h[...]
    spot = at_z * 224
    base = jnp.minimum(spot // 128 * 128, width - 384)
    row = lax.broadcasted_iota(jnp.int32, (256, 384), 0)
    lane = lax.broadcasted_iota(jnp.int32, (256, 384), 1)
    pick = jnp.where(row < 224, (row + (spot - base) == lane).astype(f32), 0.0).astype(bf16)
    placed = jnp.dot(proj[...].astype(bf16), pick, preferred_element_type=f32)
    wait_all(copies)
    total[...] = jnp.dot(act[...], weight[...], preferred_element_type=f32)
    lanes = pl.ds(offset(base, 128), 384)
    for x in range(X):
        mine = [placed[(z * X + x) * 8 : (z * X + x + 1) * 8] for z in range(Z)]
        total[x * rows : (x + 1) * rows, lanes] += jnp.concatenate(mine, axis=0)
    out[...] = total[...].astype(bf16)


def shifted(value, axis, step):
    size = lax.axis_size(axis)
    return lax.ppermute(value, axis, [(i, (i + step) % size) for i in range(size)])


def around(low, high):
    size = lax.axis_size("role") * Y
    up = [(i, (i + 1) % size) for i in range(size)]
    return (
        lax.ppermute(low, ("role", "y"), up),
        lax.ppermute(high, ("role", "y"), [(b, a) for a, b in up]),
    )


def pair(values):
    return [shifted(value, "pair", 1) for value in values]


def after(values, *others):
    return lax.optimization_barrier((values, others))[0]


def lanes(weight, begin, size):
    return lax.dynamic_slice_in_dim(weight, begin, size, 1)


def per_device(
    hidden_in,
    queries,
    new_kv,
    kv_cache,
    block_counts,
    tail_lens,
    block_order,
    out_weight,
    norm_gain,
    gate_weight,
    up_weight,
    down_weight,
):
    core, at_x, at_z, at_y = (lax.axis_index(a) for a in ("pair", "x", "z", "y"))
    at = jnp.stack([core, at_x, at_z, at_y])
    rows, width = hidden_in.shape
    slab = width // X
    block = width // (X * Z * Y)
    cols = Y * block
    chunk = X * Z * rows
    ff = gate_weight.shape[1]
    span = X * Y * ff
    heads = queries.shape[1] // X
    out_t, gate_t, up_t = out_weight.T, gate_weight.T, up_weight.T

    half = heads // 2
    pieces = [lanes(out_t, (at_x + d) % X * heads + core * half, half) for d in range(X)]
    out_pieces = [pieces[0]] + [shifted(pieces[d], "x", d) for d in range(1, X)]
    gain = shifted(norm_gain, "y", 1)
    gain = jnp.where(
        at_y == 0, jnp.concatenate([norm_gain, gain]), jnp.concatenate([gain, norm_gain])
    )[:, None]

    attended = attend(queries, new_kv, kv_cache, block_counts, tail_lens, block_order)
    first = jnp.concatenate(
        [attended.reshape(rows, X, heads), hidden_in.reshape(rows, X, slab)], axis=2
    ).transpose(1, 0, 2)
    first = after(first, (out_pieces[1], out_pieces[3], gain))
    pieces = cut(at, *after((gate_t, up_t, down_weight), first))
    first = lax.all_to_all(first, "x", 0, 0, tiled=True).reshape(X * rows, heads + slab)
    resid = first[:, heads:].reshape(X * rows, Z, cols).transpose(1, 0, 2)
    resid = jnp.pad(resid, ((0, 0), (0, 0), (0, 256 - cols)))
    first = jnp.concatenate(
        [jnp.broadcast_to(first[None, :, :heads], (Z, X * rows, heads)), resid], axis=2
    )
    first = lax.all_to_all(first, "z", 0, 0, tiled=True).reshape(chunk, heads + 256)

    out_near = join(out_pieces)
    out_side = shifted(out_near, "y", 1)
    out_all = [out_near, *pair([out_near]), out_side, *pair([out_side])]
    moved = [shifted(pieces[1], "x", 1), shifted(pieces[3], "x", -1)]
    across = shifted(after(pieces[2], moved), "x", 2)

    own, *sends = call(
        project_kernel,
        [jax.ShapeDtypeStruct((cols, chunk), t) for t in (f32, bf16, bf16, bf16)],
        [smem()] + [anywhere()] * 5,
        [
            pltpu.VMEM((X * cols, heads), bf16),
            pltpu.VMEM((chunk, heads), bf16),
            pltpu.SemaphoreType.DMA((5,)),
        ],
        (2 * X * cols * chunk * heads, X * cols * heads * 4),
        58,
    )(at, first, *out_all)
    received = [shifted(send, "x", -d) for d, send in enumerate(sends, 1)]
    weights = [join([pieces[0], moved[0]]), join([after(across, own), moved[1]])]
    weights += around(*weights)
    second, proj = call(
        norm_kernel,
        [
            jax.ShapeDtypeStruct((Z, cols + 16, chunk), bf16),
            jax.ShapeDtypeStruct((chunk, 256), f32),
        ],
        [vmem()] * 6,
        [],
        (10 * cols * chunk, 20 * cols * chunk),
        8,
    )(first, own, *received, gain)
    weights = after(weights, second)
    weights += pair(weights)
    second = lax.all_to_all(second, "z", 0, 0, tiled=True)

    message = (Z * rows, 2 * span + 128)
    own, *sends = call(
        gate_up_kernel,
        [jax.ShapeDtypeStruct(message, t) for t in (f32, bf16, bf16, bf16)],
        [smem(), vmem()] + [anywhere()] * 8,
        [
            pltpu.VMEM((2 * span, slab), bf16),
            pltpu.VMEM((slab, chunk), bf16),
            pltpu.VMEM((2 * span, chunk), f32),
            pltpu.VMEM((chunk, message[1]), f32),
            pltpu.SemaphoreType.DMA((16 + Z,)),
        ],
        (4 * span * slab * chunk, 2 * span * slab * 4),
        26,
    )(at, second, *weights)
    received = [shifted(send, "x", e) for e, send in enumerate(sends, 1)]
    hidden = call(
        lambda *refs: act_kernel(width, *refs),
        jax.ShapeDtypeStruct((Z * rows, span), bf16),
        [vmem()] * 4,
        [],
        (20 * span * Z * rows, 20 * span * Z * rows),
        8,
    )(own, *received)
    hidden = [hidden] + [shifted(hidden, "x", e) for e in range(1, X)]
    result = call(
        down_kernel,
        jax.ShapeDtypeStruct((chunk, slab), bf16),
        [smem()] + [vmem()] * 5 + [anywhere()] * 8,
        [
            pltpu.VMEM((span, slab), bf16),
            pltpu.VMEM((chunk, span), bf16),
            pltpu.VMEM((chunk, slab), f32),
            pltpu.SemaphoreType.DMA((16,)),
        ],
        (2 * span * chunk * slab, span * slab * 4),
        20,
    )(at, *hidden, proj, *weights)
    result = result.reshape(X * Z, rows, slab)
    result = lax.all_to_all(result, ("x", "z"), 0, 0, tiled=True).reshape(X, Z, rows, slab)
    result = jnp.sum(result.astype(f32), axis=1)
    result = result.transpose(1, 0, 2).reshape(rows, width)
    return (result + hidden_in.astype(f32)).astype(bf16)


def solution(mesh):
    fine = Mesh(mesh.devices.reshape(2, 2, X, Z, Y), ("role", "pair", "x", "z", "y"))
    dev = ("x", "z", "y")
    every = ("role", "pair") + dev
    return jax.shard_map(
        per_device,
        mesh=fine,
        in_specs=(
            P(every, None),
            P(every, None),
            P(every, None),
            P(every, None, None),
            P(every, None),
            P(every),
            P(every, None),
            P(None, dev),
            P(dev),
            P(None, dev),
            P(None, dev),
            P(dev, None),
        ),
        out_specs=P(every, None),
        check_vma=False,
    )
```
